512 devices in a mesh: tm: 8 (over x_hi, y), space: 64 (over x_lo, z, core).
Axes of the slice: x: 4 (x_hi: 2, x_lo: 2; x = x_hi * 2 + x_lo), y: 4, z: 16, core: 2. Of those that a mesh axis runs over, the one named last changes fastest.
Arguments:
- frames_in: bfloat16 [16, 256, 128, 256], P('tm', 'space'), may hold values from -6 to 6
- w_space: bfloat16 [9, 256, 256], replicated, may hold values from -0.125 to 0.125
- w_time: bfloat16 [3, 256, 256], replicated, may hold values from -0.21875 to 0.21875
- grad_out: bfloat16 [16, 256, 128, 256], P('tm', 'space'), may hold values from -16 to 16
Outputs:
- block_out: bfloat16 [16, 256, 128, 256], P('tm', 'space')
- grad_in: bfloat16 [16, 256, 128, 256], P('tm', 'space')
- grad_space: float32 [9, 256, 256], P(None, 'tm', 'space')
- grad_time: float32 [3, 256, 256], P(None, 'tm', 'space')
The draws below stay inside these ranges and needn't reach their ends.
All inputs are finite; a program needn't handle non-finite values.
Results may differ from the reference program's by a relative error of at most 0.0057.
Values may be sent and summed in bfloat16 or wider, within the bound.
No kernel may reach another device: no remote copies, remote signals or barrier semaphores. Data moves between devices by JAX's collectives and lax.ppermute only.
A program may use at most 64 MiB of HBM per device.

```python
import jax
import jax.numpy as jnp
from jax import lax

C = 256
COLS = 128
FRAMES = 16
ROWS = 256


def raised(values, rng, source, target, shards_of, factor):
    def block_of(dim):
        return (jnp.arange(values.shape[dim]) // (values.shape[dim] // shards_of)).reshape((-1,) + (1,) * (values.ndim - 1 - dim))

    near = jax.random.permutation(rng, shards_of)[block_of(target)]
    other_side = (block_of(target) + shards_of // 2) % shards_of
    return jnp.where((block_of(source) == near) | (block_of(source) == other_side), factor * values, values)


def steps_of(rng, dims, pieces, smallest, high):
    loudness, own = 1.0, jax.random.fold_in(rng, 6)
    for dim, blocks in pieces:
        steps = jnp.exp(jax.random.uniform(jax.random.fold_in(own, dim), (blocks,), jnp.float32, smallest / len(pieces), high / len(pieces)))
        loudness = loudness * jnp.repeat(steps, dims[dim] // blocks).reshape([-1 if axis == dim else 1 for axis in range(len(dims))])
    return loudness


def centred(own_key, extent, scale, reach, pieces=(), dtype=jnp.bfloat16):
    values = scale * jax.random.normal(own_key, extent, jnp.float32)
    if pieces:
        values = values * steps_of(own_key, extent, pieces, -0.22, 0.18)
    return jnp.clip(values, -reach, reach).astype(dtype)


def bell_draw_with(key, extent, spread, most, split, heavy, kind=jnp.bfloat16):
    drawn = spread * jax.random.normal(key, extent, jnp.float32)
    if split:
        drawn = drawn * steps_of(key, extent, split, -0.22, 0.18)
    return jnp.clip(raised(drawn, jax.random.fold_in(key, 3), *heavy), -most, most).astype(kind)


def setup_inputs(seed: int = 0) -> dict:
    streams_of = jax.random.split(jax.random.key(seed), 5)
    return {
        "frames_in": centred(streams_of[0], (FRAMES, ROWS, COLS, C), 1.0, 6.0, ((0, 8), (1, 64))),
        "w_space": centred(streams_of[1], (9, C, C), (9 * C) ** -0.5, 0.125),
        "w_time": centred(streams_of[2], (3, C, C), (3 * C) ** -0.5, 0.21875),
        "grad_out": bell_draw_with(streams_of[3], (FRAMES, ROWS, COLS, C), 1.0, 16.0, ((0, 8), (1, 64)), (1, 3, 64, 4.0)),
    }


def conv_frame(frame, w_space):
    height, width, chans = frame.shape
    padded = jnp.pad(frame, ((1, 1), (1, 1), (0, 0)))
    total = jnp.zeros((height * width, chans), jnp.float32)
    for i in range(3):
        for j in range(3):
            window = padded[i:i + height, j:j + width].reshape(-1, chans)
            total = total + jnp.dot(window, w_space[3 * i + j], preferred_element_type=jnp.float32)
    return total.reshape(height, width, chans)


def conv_back_frame(grad, w_space):
    height, width, chans = grad.shape
    padded = jnp.pad(grad, ((1, 1), (1, 1), (0, 0)))
    total = jnp.zeros((height * width, chans), jnp.float32)
    for i in range(3):
        for j in range(3):
            window = padded[2 - i:2 - i + height, 2 - j:2 - j + width].reshape(-1, chans)
            total = total + lax.dot_general(window, w_space[3 * i + j], (((1,), (1,)), ((), ())), preferred_element_type=jnp.float32)
    return total.reshape(height, width, chans)


def filter_frame(pair):
    frame, grad = pair
    height, width, chans = frame.shape
    padded = jnp.pad(frame, ((1, 1), (1, 1), (0, 0)))
    flat_grad = grad.reshape(-1, chans)
    parts = []
    for i in range(3):
        for j in range(3):
            window = padded[i:i + height, j:j + width].reshape(-1, chans)
            parts.append(lax.dot_general(window, flat_grad, (((0,), (0,)), ((), ())), preferred_element_type=jnp.float32))
    return jnp.stack(parts)


def temporal(past_ext, grad_ext, w_time, count):
    chans = past_ext.shape[-1]
    shape = grad_ext[0:count].shape
    flat_grad = grad_ext[0:count].reshape(-1, chans)
    out_sum = jnp.zeros(flat_grad.shape, jnp.float32)
    back_sum = jnp.zeros(flat_grad.shape, jnp.float32)
    filters = []
    for k in range(3):
        source = past_ext[k:k + count].reshape(-1, chans)
        out_sum = out_sum + jnp.dot(source, w_time[k], preferred_element_type=jnp.float32)
        later = grad_ext[2 - k:2 - k + count].reshape(-1, chans)
        back_sum = back_sum + lax.dot_general(later, w_time[k], (((1,), (1,)), ((), ())), preferred_element_type=jnp.float32)
        filters.append(lax.dot_general(source, flat_grad, (((0,), (0,)), ((), ())), preferred_element_type=jnp.float32))
    return out_sum.reshape(shape).astype(jnp.bfloat16), back_sum.reshape(shape).astype(jnp.bfloat16), jnp.stack(filters)


def reference(frames_in, w_space, w_time, grad_out):
    pre = lax.map(lambda frame: conv_frame(frame, w_space), frames_in)
    hidden = jax.nn.silu(pre).astype(jnp.bfloat16)
    blank = jnp.zeros((2,) + hidden.shape[1:], jnp.bfloat16)
    past_ext = jnp.concatenate([blank, hidden], axis=0)
    grad_ext = jnp.concatenate([grad_out, blank], axis=0)
    block_out, grad_hidden, grad_time = temporal(past_ext, grad_ext, w_time, hidden.shape[0])
    sig = jax.nn.sigmoid(pre)
    grad_pre = (grad_hidden.astype(jnp.float32) * sig * (1.0 + pre * (1.0 - sig))).astype(jnp.bfloat16)
    grad_in = lax.map(lambda grad: conv_back_frame(grad, w_space), grad_pre).astype(jnp.bfloat16)
    grad_space = jnp.sum(lax.map(filter_frame, (frames_in, grad_pre)), axis=0)
    return block_out, grad_in, grad_space, grad_time
```

```python
import jax
import jax.numpy as jnp
from jax import lax
from jax.experimental import pallas as pl
from jax.experimental.pallas import tpu as pltpu
from jax.sharding import Mesh
from jax.sharding import PartitionSpec as P

F32 = jnp.float32
BF16 = jnp.bfloat16
C = 256
COLS = 128
ROWS = 4
PIX = ROWS * COLS
TAPS = 12
VMEM_LIMIT = 48 * 1024 * 1024


def mm(a, b):
    return jnp.dot(a, b, preferred_element_type=F32)


def mm_t(a, b):
    return lax.dot_general(a, b, (((1,), (1,)), ((), ())), preferred_element_type=F32)


def column(shape):
    return lax.broadcasted_iota(jnp.int32, shape, 0) % COLS


def from_left(field):
    return jnp.where(column(field.shape) == 0, 0.0, pltpu.roll(field, 1, 0))


def from_right(field):
    return jnp.where(
        column(field.shape) == COLS - 1, 0.0, pltpu.roll(field, field.shape[0] - 1, 0)
    )


def shifted_transposes(pixels):
    wide = pixels.astype(F32)
    return [
        from_left(wide).astype(BF16).T,
        pixels.T,
        from_right(wide).astype(BF16).T,
    ]


def call(kernel, out_shape, flops, nbytes, *args):
    return pl.pallas_call(
        kernel,
        out_shape=out_shape,
        in_specs=[pl.BlockSpec(memory_space=pltpu.VMEM)] * len(args),
        out_specs=jax.tree.map(lambda _: pl.BlockSpec(memory_space=pltpu.VMEM), out_shape),
        compiler_params=pltpu.CompilerParams(vmem_limit_bytes=VMEM_LIMIT),
        cost_estimate=pl.CostEstimate(flops=flops, bytes_accessed=nbytes, transcendentals=0),
    )(*args)


def shape(dims, dtype):
    return jax.ShapeDtypeStruct(dims, dtype)


TAP_FLOPS = 2 * 2 * PIX * C * C


def own_kernel(x, g, ws, wt, pm, pre_ref, gh_ref, xt_ref, gp_ref):
    for f in range(2):
        for j in range(3):
            mid = mm(x[f].reshape(PIX, C), ws[3 + j])
            up = mm(x[f, 0:3].reshape(3 * COLS, C), ws[j])
            down = mm(x[f, 1:4].reshape(3 * COLS, C), ws[6 + j])
            zero = jnp.zeros((COLS, C), F32)
            total = (
                mid + jnp.concatenate([zero, up], 0) + jnp.concatenate([down, zero], 0)
            )
            if j == 0:
                acc = from_left(total)
            elif j == 1:
                acc = acc + total
            else:
                acc = acc + from_right(total)
        pre_ref[f] = acc
        for j, t in enumerate(shifted_transposes(x[f].reshape(PIX, C))):
            xt_ref[j, f] = t
        gp_ref[f] = mm(g[f].reshape(PIX, C), pm[...]).astype(BF16)
    g0, g1 = g[0].reshape(PIX, C), g[1].reshape(PIX, C)
    gh_ref[0] = mm_t(g0, wt[2]) + mm_t(g1, wt[1])
    gh_ref[1] = mm_t(g1, wt[2])


def edge_kernel(pre, lo, hi, ws, gp, hid_ref, fac_ref, ht_ref, xe_ref, gt_ref):
    for f in range(2):
        low, high = lo[f, 0], hi[f, 0]
        top = from_left(mm(low, ws[0])) + mm(low, ws[1]) + from_right(mm(low, ws[2]))
        end = from_left(mm(high, ws[6])) + mm(high, ws[7]) + from_right(mm(high, ws[8]))
        value = jnp.concatenate(
            [
                pre[f, 0:COLS] + top,
                pre[f, COLS : 3 * COLS],
                pre[f, 3 * COLS :] + end,
            ],
            0,
        )
        sig = jax.nn.sigmoid(value)
        hidden = (value * sig).astype(BF16)
        hid_ref[f] = hidden.reshape(ROWS, COLS, C)
        fac_ref[f] = sig * (1.0 + value * (1.0 - sig))
        ht_ref[f] = hidden.T
        lows, highs = shifted_transposes(low), shifted_transposes(high)
        for j in range(3):
            xe_ref[j, f, 0] = lows[j]
            xe_ref[j, f, 1] = highs[j]
    gt_ref[0] = mm(ht_ref[0], gp[1])
    gt_ref[1] = mm(ht_ref[0], gp[0]) + mm(ht_ref[1], gp[1])


def grad_kernel(n0, n1, gh, fac, xt, xe, ht, gt, wt, pm, gpre_ref, keep_ref, send_ref):
    def store(tap, value):
        keep_ref[tap] = value[:, : C // 2]
        send_ref[tap] = value[:, C // 2 :].astype(BF16)

    a0, a1 = n0[0].reshape(PIX, C), n1[0].reshape(PIX, C)
    back0 = gh[0] + mm_t(a0, wt[0])
    back1 = gh[1] + mm_t(a0, wt[1]) + mm_t(a1, wt[0])
    grads = []
    for f, back in enumerate((back0, back1)):
        gpre = (back.astype(BF16).astype(F32) * fac[f]).astype(BF16)
        gpre_ref[f] = gpre.reshape(ROWS, COLS, C)
        grads.append(mm(gpre, pm[...]).astype(BF16))
    p0 = mm(a0, pm[...]).astype(BF16)
    p1 = mm(a1, pm[...]).astype(BF16)
    store(9, mm(ht[0], p0) + mm(ht[1], p1))
    store(10, gt[0] + mm(ht[1], p0))
    store(11, gt[1])
    for j in range(3):
        for i in range(3):
            total = None
            for f in range(2):
                own = xt[j, f]
                if i == 0:
                    own = jnp.concatenate([xe[j, f, 0], own[:, : 3 * COLS]], 1)
                elif i == 2:
                    own = jnp.concatenate([own[:, COLS:], xe[j, f, 1]], 1)
                part = mm(own, grads[f])
                total = part if total is None else total + part
            store(3 * i + j, total)


def pair_kernel(keep, got, out_ref):
    half = C // 4
    for p in range(TAPS // 2):
        s0 = keep[2 * p] + got[2 * p].astype(F32)
        s1 = keep[2 * p + 1] + got[2 * p + 1].astype(F32)
        low = jnp.concatenate([s0[:, :half], s1[:, :half]], 1).astype(BF16)
        high = jnp.concatenate([s0[:, half:], s1[:, half:]], 1).astype(BF16)
        for a in range(8):
            out_ref[2 * a, :, p * 128 : (p + 1) * 128] = low[32 * a : 32 * a + 32]
            out_ref[2 * a + 1, :, p * 128 : (p + 1) * 128] = high[32 * a : 32 * a + 32]


def plane_kernel(got, out_ref):
    total = got[0].astype(F32)
    for n in range(1, 16):
        total = total + got[n].astype(F32)
    pieces = []
    for p in range(TAPS // 2):
        flipped = total[:, p * 128 : (p + 1) * 128].T
        pieces += [flipped[:64], flipped[64:]]
    wide = jnp.concatenate(pieces, 1)
    for z in range(16):
        out_ref[z] = wide[4 * z : 4 * z + 4]


def last_kernel(got, gs_ref, gt_ref):
    total = got[0]
    for n in range(1, 16):
        total = total + got[n]
    for t in range(9):
        gs_ref[t] = total[:, 32 * t : 32 * t + 32]
    for t in range(3):
        gt_ref[t] = total[:, 32 * (9 + t) : 32 * (9 + t) + 32]


def out_kernel(hid, past, wt, out_ref):
    h0, h1 = hid[0].reshape(PIX, C), hid[1].reshape(PIX, C)
    p0, p1 = past[0].reshape(PIX, C), past[1].reshape(PIX, C)
    first = mm(p0, wt[0]) + mm(p1, wt[1]) + mm(h0, wt[2])
    out_ref[0] = first.astype(BF16).reshape(ROWS, COLS, C)
    second = mm(p1, wt[0]) + mm(h0, wt[1]) + mm(h1, wt[2])
    out_ref[1] = second.astype(BF16).reshape(ROWS, COLS, C)


def back_kernel(gpre, lo, hi, ws, out_ref):
    for f in range(2):
        own = gpre[f].reshape(PIX, C)
        after = jnp.concatenate([own[COLS:], hi[f, 0]], 0)
        before = jnp.concatenate([lo[f, 0], own[: 3 * COLS]], 0)
        sums = [
            mm_t(after, ws[j]) + mm_t(own, ws[3 + j]) + mm_t(before, ws[6 + j])
            for j in range(3)
        ]
        total = from_right(sums[0]) + sums[1] + from_left(sums[2])
        out_ref[f] = total.astype(BF16).reshape(ROWS, COLS, C)


SPACE = ("xl", "z", "c")


def steps(count):
    forward = [(i, i + 1) for i in range(count - 1)]
    return forward, [(b, a) for a, b in forward]


def edges(field):
    forward, backward = steps(64)
    low = lax.ppermute(field[:, ROWS - 1 :], SPACE, forward)
    high = lax.ppermute(field[:, :1], SPACE, backward)
    return low, high


def body(frames_in, w_space, w_time, grad_out):
    forward, backward = steps(8)
    row = lax.broadcasted_iota(jnp.int32, (C, C), 0)
    col = lax.broadcasted_iota(jnp.int32, (C, C), 1)
    core = (col // 128) ^ lax.axis_index("c")
    source = ((col % 128) // 64) * 128 + ((col % 64) // 4) * 8 + core * 4 + col % 4
    order = (row == source).astype(BF16)

    low, high = edges(frames_in)
    next0 = lax.ppermute(grad_out[:1], "tm", backward)
    next1 = lax.ppermute(grad_out[1:], "tm", backward)
    pre_part, gh_part, xt, gp = call(
        own_kernel,
        (
            shape((2, PIX, C), F32),
            shape((2, PIX, C), F32),
            shape((3, 2, C, PIX), BF16),
            shape((2, PIX, C), BF16),
        ),
        12 * TAP_FLOPS,
        8 << 20,
        frames_in, grad_out, w_space, w_time, order,
    )
    hidden, factor, ht, xe, gt_part = call(
        edge_kernel,
        (
            shape((2, ROWS, COLS, C), BF16),
            shape((2, PIX, C), F32),
            shape((2, C, PIX), BF16),
            shape((3, 2, 2, C, COLS), BF16),
            shape((2, C, C), F32),
        ),
        5 * TAP_FLOPS,
        8 << 20,
        pre_part, low, high, w_space, gp,
    )
    past = lax.ppermute(hidden, "tm", forward)
    grad_pre, keep, send = call(
        grad_kernel,
        (
            shape((2, ROWS, COLS, C), BF16),
            shape((TAPS, C, C // 2), F32),
            shape((TAPS, C, C // 2), BF16),
        ),
        15 * TAP_FLOPS,
        10 << 20,
        next0, next1, gh_part, factor, xt, xe, ht, gt_part, w_time, order,
    )
    got = lax.ppermute(send, "c", [(0, 1), (1, 0)])
    chunks = call(pair_kernel, shape((16, 32, 768), BF16), 1 << 20, 4 << 20, keep, got)
    chunks = lax.all_to_all(chunks, ("tm", "xl"), split_axis=0, concat_axis=0, tiled=True)
    rows = call(plane_kernel, shape((16, 4, 384), F32), 1 << 20, 1 << 20, chunks)
    rows = lax.all_to_all(rows, "z", split_axis=0, concat_axis=0, tiled=True)
    grad_space, grad_time = call(
        last_kernel, (shape((9, 4, 32), F32), shape((3, 4, 32), F32)), 1 << 16, 1 << 18, rows
    )
    block_out = call(
        out_kernel,
        shape((2, ROWS, COLS, C), BF16),
        3 * TAP_FLOPS,
        2 << 20,
        hidden, past, w_time,
    )
    g_low, g_high = edges(grad_pre)
    grad_in = call(
        back_kernel,
        shape((2, ROWS, COLS, C), BF16),
        9 * TAP_FLOPS,
        4 << 20,
        grad_pre, g_low, g_high, w_space,
    )
    return (
        block_out,
        grad_in,
        jnp.transpose(grad_space, (0, 2, 1)),
        jnp.transpose(grad_time, (0, 2, 1)),
    )


def solution(mesh):
    fine = Mesh(mesh.devices.reshape(8, 2, 16, 2), ("tm",) + SPACE)
    in_specs = (P("tm", SPACE, None, None), P(), P(), P("tm", SPACE, None, None))
    out_specs = (
        P("tm", SPACE, None, None),
        P("tm", SPACE, None, None),
        P(None, "tm", SPACE),
        P(None, "tm", SPACE),
    )
    return jax.shard_map(body, mesh=fine, in_specs=in_specs, out_specs=out_specs, check_vma=False)
```

```python
import jax
import jax.numpy as jnp
from jax import lax
from jax.experimental import pallas as pl
from jax.experimental.pallas import tpu as pltpu
from jax.sharding import Mesh
from jax.sharding import PartitionSpec as P

F32 = jnp.float32
BF16 = jnp.bfloat16
C = 256
COLS = 128
ROWS = 4
PIX = ROWS * COLS
TAPS = 12
VMEM_LIMIT = 16 * 1024 * 1024


def mm(a, b):
    return jnp.dot(a, b, preferred_element_type=F32)


def mm_t(a, b):
    return lax.dot_general(a, b, (((1,), (1,)), ((), ())), preferred_element_type=F32)


def column(shape):
    return lax.broadcasted_iota(jnp.int32, shape, 0) % COLS


def from_left(field):
    return jnp.where(column(field.shape) == 0, 0.0, pltpu.roll(field, 1, 0))


def from_right(field):
    return jnp.where(
        column(field.shape) == COLS - 1, 0.0, pltpu.roll(field, field.shape[0] - 1, 0)
    )


def shifted_transposes(pixels):
    wide = pixels.astype(F32)
    return [
        from_left(wide).astype(BF16).T,
        pixels.T,
        from_right(wide).astype(BF16).T,
    ]


def place(arg):
    return pltpu.SMEM if arg.dtype == jnp.int32 else pltpu.VMEM


def call(kernel, out_shape, flops, nbytes, *args):
    return pl.pallas_call(
        kernel,
        out_shape=out_shape,
        in_specs=[pl.BlockSpec(memory_space=place(arg)) for arg in args],
        out_specs=jax.tree.map(lambda _: pl.BlockSpec(memory_space=pltpu.VMEM), out_shape),
        compiler_params=pltpu.CompilerParams(vmem_limit_bytes=VMEM_LIMIT),
        cost_estimate=pl.CostEstimate(flops=flops, bytes_accessed=nbytes, transcendentals=0),
    )(*args)


def shape(dims, dtype):
    return jax.ShapeDtypeStruct(dims, dtype)


TAP_FLOPS = 2 * 2 * PIX * C * C


def send_kernel(core, x, g, pair_ref, chip_ref, g0_ref, g1_ref, sems):
    c = core[0]
    copies = [
        pltpu.make_async_copy(g.at[0:1], g0_ref, sems.at[0]),
        pltpu.make_async_copy(g.at[1:2], g1_ref, sems.at[1]),
        pltpu.make_async_copy(x.at[:, pl.ds(3 - 3 * c, 1)], pair_ref, sems.at[2]),
        pltpu.make_async_copy(x.at[:, pl.ds(3 * c, 1)], chip_ref, sems.at[3]),
    ]
    for copy in copies:
        copy.start()
    for copy in copies:
        copy.wait()


def first_sends(core, x, g):
    rows = shape((2, 1, COLS, C), BF16)
    frame = shape((1, ROWS, COLS, C), BF16)
    whole = pl.BlockSpec(memory_space=pl.ANY)
    return pl.pallas_call(
        send_kernel,
        out_shape=(rows, rows, frame, frame),
        in_specs=[pl.BlockSpec(memory_space=pltpu.SMEM), whole, whole],
        out_specs=[pl.BlockSpec(memory_space=pltpu.VMEM)] * 4,
        scratch_shapes=[pltpu.SemaphoreType.DMA((4,))],
        compiler_params=pltpu.CompilerParams(vmem_limit_bytes=VMEM_LIMIT),
        cost_estimate=pl.CostEstimate(flops=0, bytes_accessed=2 << 20, transcendentals=0),
    )(core, x, g)


def low_high(core, pair, chip):
    first = core[0] == 0
    return jnp.where(first, chip, pair), jnp.where(first, pair, chip)


def own_kernel(x, g, ws, wt, pm, pre_ref, gh_ref, xt_ref, gp_ref):
    for f in range(2):
        for j in range(3):
            mid = mm(x[f].reshape(PIX, C), ws[3 + j])
            up = mm(x[f, 0:3].reshape(3 * COLS, C), ws[j])
            down = mm(x[f, 1:4].reshape(3 * COLS, C), ws[6 + j])
            zero = jnp.zeros((COLS, C), F32)
            total = (
                mid + jnp.concatenate([zero, up], 0) + jnp.concatenate([down, zero], 0)
            )
            if j == 0:
                acc = from_left(total)
            elif j == 1:
                acc = acc + total
            else:
                acc = acc + from_right(total)
        pre_ref[f] = acc
        for j, t in enumerate(shifted_transposes(x[f].reshape(PIX, C))):
            xt_ref[j, f] = t
        gp_ref[f] = mm(g[f].reshape(PIX, C), pm[...]).astype(BF16)
    g0, g1 = g[0].reshape(PIX, C), g[1].reshape(PIX, C)
    gh_ref[0] = mm_t(g0, wt[2]) + mm_t(g1, wt[1])
    gh_ref[1] = mm_t(g1, wt[2])


def edge_kernel(core, pre, pair, chip, ws, gp, hid_ref, fac_ref, ht_ref, xe_ref, gt_ref):
    for f in range(2):
        low, high = low_high(core, pair[f, 0], chip[f, 0])
        top = from_left(mm(low, ws[0])) + mm(low, ws[1]) + from_right(mm(low, ws[2]))
        end = from_left(mm(high, ws[6])) + mm(high, ws[7]) + from_right(mm(high, ws[8]))
        value = jnp.concatenate(
            [
                pre[f, 0:COLS] + top,
                pre[f, COLS : 3 * COLS],
                pre[f, 3 * COLS :] + end,
            ],
            0,
        )
        sig = jax.nn.sigmoid(value)
        hidden = (value * sig).astype(BF16)
        hid_ref[f] = hidden.reshape(ROWS, COLS, C)
        fac_ref[f] = sig * (1.0 + value * (1.0 - sig))
        ht_ref[f] = hidden.T
        lows, highs = shifted_transposes(low), shifted_transposes(high)
        for j in range(3):
            xe_ref[j, f, 0] = lows[j]
            xe_ref[j, f, 1] = highs[j]
    gt_ref[0] = mm(ht_ref[0], gp[1])
    gt_ref[1] = mm(ht_ref[0], gp[0]) + mm(ht_ref[1], gp[1])


def grad_kernel(
    core, n0, n1, gh, fac, xt, xe, ht, gt, wt, pm, gpre_ref, pair_ref, chip_ref, keep_ref, send_ref
):
    def store(tap, value):
        keep_ref[tap] = value[:, : C // 2]
        send_ref[tap] = value[:, C // 2 :].astype(BF16)

    a0, a1 = n0[0].reshape(PIX, C), n1[0].reshape(PIX, C)
    back0 = gh[0] + mm_t(a0, wt[0])
    back1 = gh[1] + mm_t(a0, wt[1]) + mm_t(a1, wt[0])
    grads = []
    for f, back in enumerate((back0, back1)):
        gpre = (back.astype(BF16).astype(F32) * fac[f]).astype(BF16)
        gpre_ref[f] = gpre.reshape(ROWS, COLS, C)
        pair_ref[f, 0] = gpre_ref[f, 3 - 3 * core[0]]
        chip_ref[f, 0] = gpre_ref[f, 3 * core[0]]
        grads.append(mm(gpre, pm[...]).astype(BF16))
    p0 = mm(a0, pm[...]).astype(BF16)
    p1 = mm(a1, pm[...]).astype(BF16)
    store(9, mm(ht[0], p0) + mm(ht[1], p1))
    store(10, gt[0] + mm(ht[1], p0))
    store(11, gt[1])
    for j in range(3):
        for i in range(3):
            total = None
            for f in range(2):
                own = xt[j, f]
                if i == 0:
                    own = jnp.concatenate([xe[j, f, 0], own[:, : 3 * COLS]], 1)
                elif i == 2:
                    own = jnp.concatenate([own[:, COLS:], xe[j, f, 1]], 1)
                part = mm(own, grads[f])
                total = part if total is None else total + part
            store(3 * i + j, total)


def pair_kernel(keep, got, out_ref):
    half = C // 4
    for p in range(TAPS // 2):
        s0 = keep[2 * p] + got[2 * p].astype(F32)
        s1 = keep[2 * p + 1] + got[2 * p + 1].astype(F32)
        low = jnp.concatenate([s0[:, :half], s1[:, :half]], 1).astype(BF16)
        high = jnp.concatenate([s0[:, half:], s1[:, half:]], 1).astype(BF16)
        for a in range(8):
            out_ref[2 * a, :, p * 128 : (p + 1) * 128] = low[32 * a : 32 * a + 32]
            out_ref[2 * a + 1, :, p * 128 : (p + 1) * 128] = high[32 * a : 32 * a + 32]


def plane_kernel(got, out_ref):
    total = got[0].astype(F32)
    for n in range(1, 16):
        total = total + got[n].astype(F32)
    pieces = []
    for p in range(TAPS // 2):
        flipped = total[:, p * 128 : (p + 1) * 128].T
        pieces += [flipped[:64], flipped[64:]]
    wide = jnp.concatenate(pieces, 1)
    for z in range(16):
        out_ref[z] = wide[4 * z : 4 * z + 4]


def last_kernel(got, gs_ref, gt_ref):
    total = got[0]
    for n in range(1, 16):
        total = total + got[n]
    for t in range(9):
        gs_ref[t] = total[:, 32 * t : 32 * t + 32]
    for t in range(3):
        gt_ref[t] = total[:, 32 * (9 + t) : 32 * (9 + t) + 32]


def out_kernel(hid, past, wt, out_ref):
    h0, h1 = hid[0].reshape(PIX, C), hid[1].reshape(PIX, C)
    p0, p1 = past[0].reshape(PIX, C), past[1].reshape(PIX, C)
    first = mm(p0, wt[0]) + mm(p1, wt[1]) + mm(h0, wt[2])
    out_ref[0] = first.astype(BF16).reshape(ROWS, COLS, C)
    second = mm(p1, wt[0]) + mm(h0, wt[1]) + mm(h1, wt[2])
    out_ref[1] = second.astype(BF16).reshape(ROWS, COLS, C)


def back_kernel(core, gpre, pair, chip, ws, out_ref):
    for f in range(2):
        low, high = low_high(core, pair[f, 0], chip[f, 0])
        own = gpre[f].reshape(PIX, C)
        after = jnp.concatenate([own[COLS:], high], 0)
        before = jnp.concatenate([low, own[: 3 * COLS]], 0)
        sums = [
            mm_t(after, ws[j]) + mm_t(own, ws[3 + j]) + mm_t(before, ws[6 + j])
            for j in range(3)
        ]
        total = from_right(sums[0]) + sums[1] + from_left(sums[2])
        out_ref[f] = total.astype(BF16).reshape(ROWS, COLS, C)


SPACE = ("xl", "z", "c")


def steps(count):
    forward = [(i, i + 1) for i in range(count - 1)]
    return forward, [(b, a) for a, b in forward]


def edges(pair, chip):
    across = [(i, i + 1) for i in range(1, 63, 2)]
    pair = lax.ppermute(pair, "c", [(0, 1), (1, 0)])
    chip = lax.ppermute(chip, SPACE, across + [(b, a) for a, b in across])
    return pair, chip


def body(frames_in, w_space, w_time, grad_out):
    forward, backward = steps(8)
    row = lax.broadcasted_iota(jnp.int32, (C, C), 0)
    col = lax.broadcasted_iota(jnp.int32, (C, C), 1)
    side = (col // 128) ^ lax.axis_index("c")
    source = ((col % 128) // 64) * 128 + ((col % 64) // 4) * 8 + side * 4 + col % 4
    order = (row == source).astype(BF16)

    core = lax.axis_index("c").reshape(1)
    pair, chip, g0, g1 = first_sends(core, frames_in, grad_out)
    next0 = lax.ppermute(g0, "tm", backward)
    next1 = lax.ppermute(g1, "tm", backward)
    pair, chip = edges(pair, chip)
    pre_part, gh_part, xt, gp = call(
        own_kernel,
        (
            shape((2, PIX, C), F32),
            shape((2, PIX, C), F32),
            shape((3, 2, C, PIX), BF16),
            shape((2, PIX, C), BF16),
        ),
        12 * TAP_FLOPS,
        8 << 20,
        frames_in, grad_out, w_space, w_time, order,
    )
    hidden, factor, ht, xe, gt_part = call(
        edge_kernel,
        (
            shape((2, ROWS, COLS, C), BF16),
            shape((2, PIX, C), F32),
            shape((2, C, PIX), BF16),
            shape((3, 2, 2, C, COLS), BF16),
            shape((2, C, C), F32),
        ),
        5 * TAP_FLOPS,
        8 << 20,
        core, pre_part, pair, chip, w_space, gp,
    )
    past = lax.ppermute(hidden, "tm", forward)
    rows = shape((2, 1, COLS, C), BF16)
    grad_pre, pair, chip, keep, send = call(
        grad_kernel,
        (
            shape((2, ROWS, COLS, C), BF16),
            rows,
            rows,
            shape((TAPS, C, C // 2), F32),
            shape((TAPS, C, C // 2), BF16),
        ),
        15 * TAP_FLOPS,
        10 << 20,
        core, next0, next1, gh_part, factor, xt, xe, ht, gt_part, w_time, order,
    )
    got = lax.ppermute(send, "c", [(0, 1), (1, 0)])
    chunks = call(pair_kernel, shape((16, 32, 768), BF16), 1 << 20, 4 << 20, keep, got)
    chunks = lax.all_to_all(chunks, ("tm", "xl"), split_axis=0, concat_axis=0, tiled=True)
    block_out = call(
        out_kernel,
        shape((2, ROWS, COLS, C), BF16),
        3 * TAP_FLOPS,
        2 << 20,
        hidden, past, w_time,
    )
    pair, chip = edges(pair, chip)
    grad_in = call(
        back_kernel,
        shape((2, ROWS, COLS, C), BF16),
        9 * TAP_FLOPS,
        4 << 20,
        core, grad_pre, pair, chip, w_space,
    )
    chunks, grad_in = lax.optimization_barrier((chunks, grad_in))
    rows = call(plane_kernel, shape((16, 4, 384), F32), 1 << 20, 1 << 20, chunks)
    rows = lax.all_to_all(rows, "z", split_axis=0, concat_axis=0, tiled=True)
    grad_space, grad_time = call(
        last_kernel, (shape((9, 4, 32), F32), shape((3, 4, 32), F32)), 1 << 16, 1 << 18, rows
    )
    return (
        block_out,
        grad_in,
        jnp.transpose(grad_space, (0, 2, 1)),
        jnp.transpose(grad_time, (0, 2, 1)),
    )


def solution(mesh):
    fine = Mesh(mesh.devices.reshape(8, 2, 16, 2), ("tm",) + SPACE)
    in_specs = (P("tm", SPACE, None, None), P(), P(), P("tm", SPACE, None, None))
    out_specs = (
        P("tm", SPACE, None, None),
        P("tm", SPACE, None, None),
        P(None, "tm", SPACE),
        P(None, "tm", SPACE),
    )
    return jax.shard_map(body, mesh=fine, in_specs=in_specs, out_specs=out_specs, check_vma=False)
```

```python
import jax
import jax.numpy as jnp
from jax import lax
from jax.experimental import pallas as pl
from jax.experimental.pallas import tpu as pltpu
from jax.sharding import Mesh
from jax.sharding import PartitionSpec as P

F32 = jnp.float32
BF16 = jnp.bfloat16
C = 256
COLS = 128
ROWS = 4
PIX = ROWS * COLS
TAPS = 12
VMEM_LIMIT = 16 * 1024 * 1024
HINT = 1 << 33


def mm(a, b):
    return jnp.dot(a, b, preferred_element_type=F32)


def mm_t(a, b):
    return lax.dot_general(a, b, (((1,), (1,)), ((), ())), preferred_element_type=F32)


def column(shape):
    return lax.broadcasted_iota(jnp.int32, shape, 0) % COLS


def from_left(field):
    return jnp.where(column(field.shape) == 0, 0.0, pltpu.roll(field, 1, 0))


def from_right(field):
    return jnp.where(
        column(field.shape) == COLS - 1, 0.0, pltpu.roll(field, field.shape[0] - 1, 0)
    )


def shifted_transposes(pixels):
    wide = pixels.astype(F32)
    return [
        from_left(wide).astype(BF16).T,
        pixels.T,
        from_right(wide).astype(BF16).T,
    ]


def place(arg):
    return pltpu.SMEM if arg.dtype == jnp.int32 else pltpu.VMEM


def call(kernel, out_shape, flops, nbytes, *args, hbm_in=(), hbm_out=(), scratch=()):
    flat, tree = jax.tree.flatten(out_shape)
    out_specs = [
        pl.BlockSpec(memory_space=pltpu.HBM if n in hbm_out else pltpu.VMEM)
        for n in range(len(flat))
    ]
    in_specs = [
        pl.BlockSpec(memory_space=pltpu.HBM if n in hbm_in else place(arg))
        for n, arg in enumerate(args)
    ]
    return pl.pallas_call(
        kernel,
        out_shape=out_shape,
        in_specs=in_specs,
        out_specs=jax.tree.unflatten(tree, out_specs),
        scratch_shapes=list(scratch),
        compiler_params=pltpu.CompilerParams(vmem_limit_bytes=VMEM_LIMIT),
        cost_estimate=pl.CostEstimate(flops=flops, bytes_accessed=nbytes, transcendentals=0),
    )(*args)


def shape(dims, dtype):
    return jax.ShapeDtypeStruct(dims, dtype)


TAP_FLOPS = 2 * 2 * PIX * C * C


def order_kernel(core, out_ref):
    row = lax.broadcasted_iota(jnp.int32, (C, C), 0)
    col = lax.broadcasted_iota(jnp.int32, (C, C), 1)
    side = (col // 128) ^ core[0]
    source = ((col % 128) // 64) * 128 + ((col % 64) // 4) * 8 + side * 4 + col % 4
    out_ref[...] = jnp.where(row == source, 1.0, 0.0).astype(BF16)


def piece_kernel(g, pm, g0_ref, g1_ref, sems):
    copies = [
        pltpu.make_async_copy(g.at[0:1], g0_ref, sems.at[0]),
        pltpu.make_async_copy(g.at[1:2], g1_ref, sems.at[1]),
    ]
    for copy in copies:
        copy.start()
    for copy in copies:
        copy.wait()


def first_kernel(core, x, g, wt, pm, gh_ref, gp_ref, pair_ref, chip_ref):
    c = core[0]
    for f in range(2):
        pair_ref[f, 0] = x[f, 3 - 3 * c]
        chip_ref[f, 0] = x[f, 3 * c]
        gp_ref[f] = mm(g[f].reshape(PIX, C), pm[...]).astype(BF16)
    g0, g1 = g[0].reshape(PIX, C), g[1].reshape(PIX, C)
    gh_ref[0] = mm_t(g0, wt[2]) + mm_t(g1, wt[1])
    gh_ref[1] = mm_t(g1, wt[2])


def low_high(core, pair, chip):
    first = core[0] == 0
    return jnp.where(first, chip, pair), jnp.where(first, pair, chip)


def own_kernel(x, ws, pre_ref, xt_ref):
    for f in range(2):
        for j in range(3):
            mid = mm(x[f].reshape(PIX, C), ws[3 + j])
            up = mm(x[f, 0:3].reshape(3 * COLS, C), ws[j])
            down = mm(x[f, 1:4].reshape(3 * COLS, C), ws[6 + j])
            zero = jnp.zeros((COLS, C), F32)
            total = (
                mid + jnp.concatenate([zero, up], 0) + jnp.concatenate([down, zero], 0)
            )
            if j == 0:
                acc = from_left(total)
            elif j == 1:
                acc = acc + total
            else:
                acc = acc + from_right(total)
        pre_ref[f] = acc
        for j, t in enumerate(shifted_transposes(x[f].reshape(PIX, C))):
            xt_ref[j, f] = t


def edge_kernel(core, pre, pair, chip, ws, gp, hid_ref, fac_ref, ht_ref, xe_ref, gt_ref):
    for f in range(2):
        low, high = low_high(core, pair[f, 0], chip[f, 0])
        top = from_left(mm(low, ws[0])) + mm(low, ws[1]) + from_right(mm(low, ws[2]))
        end = from_left(mm(high, ws[6])) + mm(high, ws[7]) + from_right(mm(high, ws[8]))
        value = jnp.concatenate(
            [
                pre[f, 0:COLS] + top,
                pre[f, COLS : 3 * COLS],
                pre[f, 3 * COLS :] + end,
            ],
            0,
        )
        sig = jax.nn.sigmoid(value)
        hidden = (value * sig).astype(BF16)
        hid_ref[f] = hidden.reshape(ROWS, COLS, C)
        fac_ref[f] = sig * (1.0 + value * (1.0 - sig))
        ht_ref[f] = hidden.T
        lows, highs = shifted_transposes(low), shifted_transposes(high)
        for j in range(3):
            xe_ref[j, f, 0] = lows[j]
            xe_ref[j, f, 1] = highs[j]
    gt_ref[0] = mm(ht_ref[0], gp[1])
    gt_ref[1] = mm(ht_ref[0], gp[0]) + mm(ht_ref[1], gp[1])


def grad_kernel(
    core, n0, n1, gh, fac, xt, xe, ht, gt, wt, pm,
    gpre_hbm, pair_ref, chip_ref, keep_ref, send_ref,
    gpre_ref, sem,
):
    def store(tap, value):
        keep_ref[tap] = value[:, : C // 2]
        send_ref[tap] = value[:, C // 2 :].astype(BF16)

    a0, a1 = n0[0].reshape(PIX, C), n1[0].reshape(PIX, C)
    back0 = gh[0] + mm_t(a0, wt[0])
    back1 = gh[1] + mm_t(a0, wt[1]) + mm_t(a1, wt[0])
    grads = []
    for f, back in enumerate((back0, back1)):
        gpre = (back.astype(BF16).astype(F32) * fac[f]).astype(BF16)
        gpre_ref[f] = gpre.reshape(ROWS, COLS, C)
        pair_ref[f, 0] = gpre_ref[f, 3 - 3 * core[0]]
        chip_ref[f, 0] = gpre_ref[f, 3 * core[0]]
        grads.append(mm(gpre, pm[...]).astype(BF16))
    copy = pltpu.make_async_copy(gpre_ref, gpre_hbm, sem)
    copy.start()
    p0 = mm(a0, pm[...]).astype(BF16)
    p1 = mm(a1, pm[...]).astype(BF16)
    store(9, mm(ht[0], p0) + mm(ht[1], p1))
    store(10, gt[0] + mm(ht[1], p0))
    store(11, gt[1])
    for j in range(3):
        for i in range(3):
            total = None
            for f in range(2):
                own = xt[j, f]
                if i == 0:
                    own = jnp.concatenate([xe[j, f, 0], own[:, : 3 * COLS]], 1)
                elif i == 2:
                    own = jnp.concatenate([own[:, COLS:], xe[j, f, 1]], 1)
                part = mm(own, grads[f])
                total = part if total is None else total + part
            store(3 * i + j, total)
    copy.wait()


def pair_kernel(keep, got, out_ref):
    half = C // 4
    for p in range(TAPS // 2):
        s0 = keep[2 * p] + got[2 * p].astype(F32)
        s1 = keep[2 * p + 1] + got[2 * p + 1].astype(F32)
        low = jnp.concatenate([s0[:, :half], s1[:, :half]], 1).astype(BF16)
        high = jnp.concatenate([s0[:, half:], s1[:, half:]], 1).astype(BF16)
        for a in range(8):
            out_ref[2 * a, :, p * 128 : (p + 1) * 128] = low[32 * a : 32 * a + 32]
            out_ref[2 * a + 1, :, p * 128 : (p + 1) * 128] = high[32 * a : 32 * a + 32]


def plane_kernel(got, out_ref):
    total = got[0].astype(F32)
    for n in range(1, 16):
        total = total + got[n].astype(F32)
    pieces = []
    for p in range(TAPS // 2):
        flipped = total[:, p * 128 : (p + 1) * 128].T
        pieces += [flipped[:64], flipped[64:]]
    wide = jnp.concatenate(pieces, 1)
    for z in range(16):
        out_ref[z] = wide[4 * z : 4 * z + 4]


def last_kernel(got, gs_ref, gt_ref):
    total = got[0]
    for n in range(1, 16):
        total = total + got[n]
    for t in range(9):
        gs_ref[t] = total[:, 32 * t : 32 * t + 32]
    for t in range(3):
        gt_ref[t] = total[:, 32 * (9 + t) : 32 * (9 + t) + 32]


def out_kernel(hid, past, wt, out_ref):
    h0, h1 = hid[0].reshape(PIX, C), hid[1].reshape(PIX, C)
    p0, p1 = past[0].reshape(PIX, C), past[1].reshape(PIX, C)
    first = mm(p0, wt[0]) + mm(p1, wt[1]) + mm(h0, wt[2])
    out_ref[0] = first.astype(BF16).reshape(ROWS, COLS, C)
    second = mm(p1, wt[0]) + mm(h0, wt[1]) + mm(h1, wt[2])
    out_ref[1] = second.astype(BF16).reshape(ROWS, COLS, C)


def back_kernel(core, gpre, pair, chip, ws, out_ref):
    for f in range(2):
        low, high = low_high(core, pair[f, 0], chip[f, 0])
        own = gpre[f].reshape(PIX, C)
        after = jnp.concatenate([own[COLS:], high], 0)
        before = jnp.concatenate([low, own[: 3 * COLS]], 0)
        sums = [
            mm_t(after, ws[j]) + mm_t(own, ws[3 + j]) + mm_t(before, ws[6 + j])
            for j in range(3)
        ]
        total = from_right(sums[0]) + sums[1] + from_left(sums[2])
        out_ref[f] = total.astype(BF16).reshape(ROWS, COLS, C)


SPACE = ("xl", "z", "c")


def steps(count):
    forward = [(i, i + 1) for i in range(count - 1)]
    return forward, [(b, a) for a, b in forward]


def edges(pair, chip):
    across = [(i, i + 1) for i in range(1, 63, 2)]
    chip = lax.ppermute(chip, SPACE, across + [(b, a) for a, b in across])
    pair = lax.ppermute(pair, "c", [(0, 1), (1, 0)])
    return pair, chip


def body(frames_in, w_space, w_time, grad_out):
    forward, backward = steps(8)
    core = lax.axis_index("c").reshape(1)
    order = call(order_kernel, shape((C, C), BF16), HINT, 1 << 17, core)
    frame = shape((1, ROWS, COLS, C), BF16)
    rows = shape((2, 1, COLS, C), BF16)
    g0, g1 = call(
        piece_kernel, (frame, frame), 0, 1 << 20, grad_out, order,
        hbm_in=(0,), scratch=[pltpu.SemaphoreType.DMA((2,))],
    )
    next0 = lax.ppermute(g0, "tm", backward)
    next1 = lax.ppermute(g1, "tm", backward)
    gh_part, gp, pair, chip = call(
        first_kernel,
        (shape((2, PIX, C), F32), shape((2, PIX, C), BF16), rows, rows),
        4 * TAP_FLOPS,
        4 << 20,
        core, frames_in, grad_out, w_time, order,
    )
    pair, chip = edges(pair, chip)
    pre_part, xt = call(
        own_kernel,
        (shape((2, PIX, C), F32), shape((3, 2, C, PIX), BF16)),
        9 * TAP_FLOPS,
        4 << 20,
        frames_in, w_space,
    )
    hidden, factor, ht, xe, gt_part = call(
        edge_kernel,
        (
            shape((2, ROWS, COLS, C), BF16),
            shape((2, PIX, C), F32),
            shape((2, C, PIX), BF16),
            shape((3, 2, 2, C, COLS), BF16),
            shape((2, C, C), F32),
        ),
        5 * TAP_FLOPS,
        8 << 20,
        core, pre_part, pair, chip, w_space, gp,
    )
    grad_pre, pair, chip, keep, send = call(
        grad_kernel,
        (
            shape((2, ROWS, COLS, C), BF16),
            rows,
            rows,
            shape((TAPS, C, C // 2), F32),
            shape((TAPS, C, C // 2), BF16),
        ),
        15 * TAP_FLOPS,
        10 << 20,
        core, next0, next1, gh_part, factor, xt, xe, ht, gt_part, w_time, order,
        hbm_out=(0,),
        scratch=[pltpu.VMEM((2, ROWS, COLS, C), BF16), pltpu.SemaphoreType.DMA],
    )
    got = lax.ppermute(send, "c", [(0, 1), (1, 0)])
    chunks = call(pair_kernel, shape((16, 32, 768), BF16), 1 << 20, 4 << 20, keep, got)
    chunks = lax.all_to_all(chunks, ("tm", "xl"), split_axis=0, concat_axis=0, tiled=True)
    pair, chip = edges(pair, chip)
    chunks, pair, chip, hidden = lax.optimization_barrier((chunks, pair, chip, hidden))
    past = lax.ppermute(hidden, "tm", forward)
    block_out = call(
        out_kernel,
        shape((2, ROWS, COLS, C), BF16),
        3 * TAP_FLOPS,
        2 << 20,
        hidden, past, w_time,
    )
    grad_in = call(
        back_kernel,
        shape((2, ROWS, COLS, C), BF16),
        9 * TAP_FLOPS,
        4 << 20,
        core, grad_pre, pair, chip, w_space,
    )
    rows = call(plane_kernel, shape((16, 4, 384), F32), 1 << 20, 1 << 20, chunks)
    rows = lax.all_to_all(rows, "z", split_axis=0, concat_axis=0, tiled=True)
    rows, block_out = lax.optimization_barrier((rows, block_out))
    grad_space, grad_time = call(
        last_kernel, (shape((9, 4, 32), F32), shape((3, 4, 32), F32)), 1 << 16, 1 << 18, rows
    )
    return (
        block_out,
        grad_in,
        jnp.transpose(grad_space, (0, 2, 1)),
        jnp.transpose(grad_time, (0, 2, 1)),
    )


def solution(mesh):
    fine = Mesh(mesh.devices.reshape(8, 2, 16, 2), ("tm",) + SPACE)
    in_specs = (P("tm", SPACE, None, None), P(), P(), P("tm", SPACE, None, None))
    out_specs = (
        P("tm", SPACE, None, None),
        P("tm", SPACE, None, None),
        P(None, "tm", SPACE),
        P(None, "tm", SPACE),
    )
    return jax.shard_map(body, mesh=fine, in_specs=in_specs, out_specs=out_specs, check_vma=False)
```

```python
import jax
import jax.numpy as jnp
from jax import lax
from jax.experimental import pallas as pl
from jax.experimental.pallas import tpu as pltpu
from jax.sharding import Mesh
from jax.sharding import PartitionSpec as P

F32 = jnp.float32
BF16 = jnp.bfloat16
C = 256
COLS = 128
ROWS = 4
PIX = ROWS * COLS
TAPS = 12
VMEM_LIMIT = 16 * 1024 * 1024
HINT = 1 << 33


def mm(a, b):
    return jnp.dot(a, b, preferred_element_type=F32)


def mm_t(a, b):
    return lax.dot_general(a, b, (((1,), (1,)), ((), ())), preferred_element_type=F32)


def column(shape):
    return lax.broadcasted_iota(jnp.int32, shape, 0) % COLS


def from_left(field):
    return jnp.where(column(field.shape) == 0, 0.0, pltpu.roll(field, 1, 0))


def from_right(field):
    return jnp.where(
        column(field.shape) == COLS - 1, 0.0, pltpu.roll(field, field.shape[0] - 1, 0)
    )


def shifted_transposes(pixels):
    wide = pixels.astype(F32)
    return [
        from_left(wide).astype(BF16).T,
        pixels.T,
        from_right(wide).astype(BF16).T,
    ]


def place(arg):
    return pltpu.SMEM if arg.dtype == jnp.int32 else pltpu.VMEM


def call(kernel, out_shape, flops, nbytes, *args, hbm_in=(), hbm_out=(), scratch=()):
    flat, tree = jax.tree.flatten(out_shape, is_leaf=lambda leaf: hasattr(leaf, "dtype"))
    out_specs = [
        pl.BlockSpec(memory_space=pltpu.HBM if n in hbm_out else pltpu.VMEM)
        for n in range(len(flat))
    ]
    in_specs = [
        pl.BlockSpec(memory_space=pltpu.HBM if n in hbm_in else place(arg))
        for n, arg in enumerate(args)
    ]
    return pl.pallas_call(
        kernel,
        out_shape=out_shape,
        in_specs=in_specs,
        out_specs=jax.tree.unflatten(tree, out_specs),
        scratch_shapes=list(scratch),
        compiler_params=pltpu.CompilerParams(vmem_limit_bytes=VMEM_LIMIT),
        cost_estimate=pl.CostEstimate(flops=flops, bytes_accessed=nbytes, transcendentals=0),
    )(*args)


def shape(dims, dtype):
    return jax.ShapeDtypeStruct(dims, dtype)


def vmem(dims, dtype):
    return pltpu.VMEM(dims, dtype)


def hbm(dims, dtype):
    return pltpu.HBM(dims, dtype)


TAP_FLOPS = 2 * 2 * PIX * C * C


def order_kernel(core, out_ref):
    row = lax.broadcasted_iota(jnp.int32, (C, C), 0)
    col = lax.broadcasted_iota(jnp.int32, (C, C), 1)
    side = (col // 128) ^ core[0]
    source = ((col % 128) // 64) * 128 + ((col % 64) // 4) * 8 + side * 4 + col % 4
    out_ref[...] = jnp.where(row == source, 1.0, 0.0).astype(BF16)


def first_kernel(core, x, g, wt, pm, gh_ref, gp_ref, pair_ref, chip_ref):
    c = core[0]
    for f in range(2):
        pair_ref[f, 0] = x[f, 3 - 3 * c]
        chip_ref[f, 0] = x[f, 3 * c]
        gp_ref[f] = mm(g[f].reshape(PIX, C), pm[...]).astype(BF16)
    g0, g1 = g[0].reshape(PIX, C), g[1].reshape(PIX, C)
    gh_ref[0] = mm_t(g0, wt[2]) + mm_t(g1, wt[1])
    gh_ref[1] = mm_t(g1, wt[2])


def low_high(core, pair, chip):
    first = core[0] == 0
    return jnp.where(first, chip, pair), jnp.where(first, pair, chip)


def own_kernel(x, ws, pre_ref, xt_ref):
    for f in range(2):
        for j in range(3):
            mid = mm(x[f].reshape(PIX, C), ws[3 + j])
            up = mm(x[f, 0:3].reshape(3 * COLS, C), ws[j])
            down = mm(x[f, 1:4].reshape(3 * COLS, C), ws[6 + j])
            zero = jnp.zeros((COLS, C), F32)
            total = (
                mid + jnp.concatenate([zero, up], 0) + jnp.concatenate([down, zero], 0)
            )
            if j == 0:
                acc = from_left(total)
            elif j == 1:
                acc = acc + total
            else:
                acc = acc + from_right(total)
        pre_ref[f] = acc
        for j, t in enumerate(shifted_transposes(x[f].reshape(PIX, C))):
            xt_ref[j, f] = t


def edge_kernel(core, pre, pair, chip, ws, gp, hid_ref, fac_ref, ht_ref, xe_ref, gt_ref):
    for f in range(2):
        low, high = low_high(core, pair[f, 0], chip[f, 0])
        top = from_left(mm(low, ws[0])) + mm(low, ws[1]) + from_right(mm(low, ws[2]))
        end = from_left(mm(high, ws[6])) + mm(high, ws[7]) + from_right(mm(high, ws[8]))
        value = jnp.concatenate(
            [
                pre[f, 0:COLS] + top,
                pre[f, COLS : 3 * COLS],
                pre[f, 3 * COLS :] + end,
            ],
            0,
        )
        sig = jax.nn.sigmoid(value)
        hidden = (value * sig).astype(BF16)
        hid_ref[f] = hidden.reshape(ROWS, COLS, C)
        fac_ref[f] = sig * (1.0 + value * (1.0 - sig))
        ht_ref[f] = hidden.T
        lows, highs = shifted_transposes(low), shifted_transposes(high)
        for j in range(3):
            xe_ref[j, f, 0] = lows[j]
            xe_ref[j, f, 1] = highs[j]
    gt_ref[0] = mm(ht_ref[0], gp[1])
    gt_ref[1] = mm(ht_ref[0], gp[0]) + mm(ht_ref[1], gp[1])


def grad_kernel(
    core, n, gh, fac, xt, xe, ht, gt, wt, pm,
    gpre_hbm, pair_hbm, chip_hbm, keep_ref, send_ref,
    gpre_ref, sems,
):
    def store(tap, value):
        keep_ref[tap] = value[:, : C // 2]
        send_ref[tap] = value[:, C // 2 :].astype(BF16)

    a0, a1 = n[0].reshape(PIX, C), n[1].reshape(PIX, C)
    back0 = gh[0] + mm_t(a0, wt[0])
    back1 = gh[1] + mm_t(a0, wt[1]) + mm_t(a1, wt[0])
    grads = []
    for f, back in enumerate((back0, back1)):
        gpre = (back.astype(BF16).astype(F32) * fac[f]).astype(BF16)
        gpre_ref[f] = gpre.reshape(ROWS, COLS, C)
        grads.append(mm(gpre, pm[...]).astype(BF16))
    c = core[0]
    copies = [
        pltpu.make_async_copy(gpre_ref.at[:, pl.ds(3 - 3 * c, 1)], pair_hbm, sems.at[0]),
        pltpu.make_async_copy(gpre_ref.at[:, pl.ds(3 * c, 1)], chip_hbm, sems.at[1]),
        pltpu.make_async_copy(gpre_ref, gpre_hbm, sems.at[2]),
    ]
    for copy in copies:
        copy.start()
    p0 = mm(a0, pm[...]).astype(BF16)
    p1 = mm(a1, pm[...]).astype(BF16)
    store(9, mm(ht[0], p0) + mm(ht[1], p1))
    store(10, gt[0] + mm(ht[1], p0))
    store(11, gt[1])
    for j in range(3):
        for i in range(3):
            total = None
            for f in range(2):
                own = xt[j, f]
                if i == 0:
                    own = jnp.concatenate([xe[j, f, 0], own[:, : 3 * COLS]], 1)
                elif i == 2:
                    own = jnp.concatenate([own[:, COLS:], xe[j, f, 1]], 1)
                part = mm(own, grads[f])
                total = part if total is None else total + part
            store(3 * i + j, total)
    for copy in copies:
        copy.wait()


def pair_kernel(keep, got, out_ref):
    half = C // 4
    for p in range(TAPS // 2):
        s0 = keep[2 * p] + got[2 * p].astype(F32)
        s1 = keep[2 * p + 1] + got[2 * p + 1].astype(F32)
        low = jnp.concatenate([s0[:, :half], s1[:, :half]], 1).astype(BF16)
        high = jnp.concatenate([s0[:, half:], s1[:, half:]], 1).astype(BF16)
        for a in range(8):
            out_ref[2 * a, :, p * 128 : (p + 1) * 128] = low[32 * a : 32 * a + 32]
            out_ref[2 * a + 1, :, p * 128 : (p + 1) * 128] = high[32 * a : 32 * a + 32]


def plane_kernel(got, out_ref):
    total = got[0].astype(F32)
    for n in range(1, 16):
        total = total + got[n].astype(F32)
    pieces = []
    for p in range(TAPS // 2):
        flipped = total[:, p * 128 : (p + 1) * 128].T
        pieces += [flipped[:64], flipped[64:]]
    wide = jnp.concatenate(pieces, 1)
    for z in range(16):
        out_ref[z] = wide[4 * z : 4 * z + 4]


def last_kernel(got, gs_ref, gt_ref):
    total = got[0]
    for n in range(1, 16):
        total = total + got[n]
    for t in range(9):
        gs_ref[t] = total[:, 32 * t : 32 * t + 32]
    for t in range(3):
        gt_ref[t] = total[:, 32 * (9 + t) : 32 * (9 + t) + 32]


def out_kernel(hid, past, wt, out_ref):
    h0, h1 = hid[0].reshape(PIX, C), hid[1].reshape(PIX, C)
    p0, p1 = past[0].reshape(PIX, C), past[1].reshape(PIX, C)
    first = mm(p0, wt[0]) + mm(p1, wt[1]) + mm(h0, wt[2])
    out_ref[0] = first.astype(BF16).reshape(ROWS, COLS, C)
    second = mm(p1, wt[0]) + mm(h0, wt[1]) + mm(h1, wt[2])
    out_ref[1] = second.astype(BF16).reshape(ROWS, COLS, C)


def back_kernel(core, gpre, pair, chip, ws, out_ref):
    for f in range(2):
        low, high = low_high(core, pair[f, 0], chip[f, 0])
        own = gpre[f].reshape(PIX, C)
        after = jnp.concatenate([own[COLS:], high], 0)
        before = jnp.concatenate([low, own[: 3 * COLS]], 0)
        sums = [
            mm_t(after, ws[j]) + mm_t(own, ws[3 + j]) + mm_t(before, ws[6 + j])
            for j in range(3)
        ]
        total = from_right(sums[0]) + sums[1] + from_left(sums[2])
        out_ref[f] = total.astype(BF16).reshape(ROWS, COLS, C)


SPACE = ("xl", "z", "c")


def steps(count):
    forward = [(i, i + 1) for i in range(count - 1)]
    return forward, [(b, a) for a, b in forward]


def to_pair(rows):
    return lax.ppermute(rows, "c", [(0, 1), (1, 0)])


def to_chip(rows):
    across = [(i, i + 1) for i in range(1, 63, 2)]
    return lax.ppermute(rows, SPACE, across + [(b, a) for a, b in across])


def body(frames_in, w_space, w_time, grad_out):
    forward, backward = steps(8)
    core = lax.axis_index("c").reshape(1)
    order = call(order_kernel, shape((C, C), BF16), HINT, 1 << 17, core)
    rows = shape((2, 1, COLS, C), BF16)
    later = lax.ppermute(grad_out, "tm", backward)
    gh_part, gp, pair, chip = call(
        first_kernel,
        (shape((2, PIX, C), F32), shape((2, PIX, C), BF16), rows, rows),
        4 * TAP_FLOPS,
        4 << 20,
        core, frames_in, grad_out, w_time, order,
    )
    pair, chip = to_pair(pair), to_chip(chip)
    pre_part, xt = call(
        own_kernel,
        (shape((2, PIX, C), F32), shape((3, 2, C, PIX), BF16)),
        9 * TAP_FLOPS,
        4 << 20,
        frames_in, w_space,
    )
    hidden, factor, ht, xe, gt_part = call(
        edge_kernel,
        (
            shape((2, ROWS, COLS, C), BF16),
            shape((2, PIX, C), F32),
            shape((2, C, PIX), BF16),
            shape((3, 2, 2, C, COLS), BF16),
            shape((2, C, C), F32),
        ),
        5 * TAP_FLOPS,
        8 << 20,
        core, pre_part, pair, chip, w_space, gp,
    )
    grad_pre, pair, chip, keep, send = call(
        grad_kernel,
        (
            hbm((2, ROWS, COLS, C), BF16),
            hbm((2, 1, COLS, C), BF16),
            hbm((2, 1, COLS, C), BF16),
            vmem((TAPS, C, C // 2), F32),
            vmem((TAPS, C, C // 2), BF16),
        ),
        15 * TAP_FLOPS,
        10 << 20,
        core, later, gh_part, factor, xt, xe, ht, gt_part, w_time, order,
        hbm_out=(0, 1, 2),
        scratch=[pltpu.VMEM((2, ROWS, COLS, C), BF16), pltpu.SemaphoreType.DMA((3,))],
    )
    got = lax.ppermute(send, "c", [(0, 1), (1, 0)])
    chunks = call(pair_kernel, shape((16, 32, 768), BF16), 1 << 20, 4 << 20, keep, got)
    chunks = lax.all_to_all(chunks, ("tm", "xl"), split_axis=0, concat_axis=0, tiled=True)
    pair = to_pair(pair)
    chip, pair = lax.optimization_barrier((chip, pair))
    chip = to_chip(chip)
    hidden, chip = lax.optimization_barrier((hidden, chip))
    past = lax.ppermute(hidden, "tm", forward)
    chunks, pair, chip = lax.optimization_barrier((chunks, pair, chip))
    block_out = call(
        out_kernel,
        shape((2, ROWS, COLS, C), BF16),
        3 * TAP_FLOPS,
        2 << 20,
        hidden, past, w_time,
    )
    grad_in = call(
        back_kernel,
        shape((2, ROWS, COLS, C), BF16),
        9 * TAP_FLOPS,
        4 << 20,
        core, grad_pre, pair, chip, w_space,
    )
    rows = call(plane_kernel, shape((16, 4, 384), F32), 1 << 20, 1 << 20, chunks)
    rows = lax.all_to_all(rows, "z", split_axis=0, concat_axis=0, tiled=True)
    rows, block_out = lax.optimization_barrier((rows, block_out))
    grad_space, grad_time = call(
        last_kernel, (shape((9, 4, 32), F32), shape((3, 4, 32), F32)), 1 << 16, 1 << 18, rows
    )
    return (
        block_out,
        grad_in,
        jnp.transpose(grad_space, (0, 2, 1)),
        jnp.transpose(grad_time, (0, 2, 1)),
    )


def solution(mesh):
    fine = Mesh(mesh.devices.reshape(8, 2, 16, 2), ("tm",) + SPACE)
    in_specs = (P("tm", SPACE, None, None), P(), P(), P("tm", SPACE, None, None))
    out_specs = (
        P("tm", SPACE, None, None),
        P("tm", SPACE, None, None),
        P(None, "tm", SPACE),
        P(None, "tm", SPACE),
    )
    return jax.shard_map(body, mesh=fine, in_specs=in_specs, out_specs=out_specs, check_vma=False)
```

```python
import jax
import jax.numpy as jnp
from jax import lax
from jax.experimental import pallas as pl
from jax.experimental.pallas import tpu as pltpu
from jax.sharding import Mesh
from jax.sharding import PartitionSpec as P

F32 = jnp.float32
BF16 = jnp.bfloat16
C = 256
COLS = 128
ROWS = 4
PIX = ROWS * COLS
TAPS = 12
VMEM_LIMIT = 16 * 1024 * 1024
HINT = 1 << 33


def mm(a, b):
    return jnp.dot(a, b, preferred_element_type=F32)


def mm_t(a, b):
    return lax.dot_general(a, b, (((1,), (1,)), ((), ())), preferred_element_type=F32)


def column(shape):
    return lax.broadcasted_iota(jnp.int32, shape, 0) % COLS


def from_left(field):
    return jnp.where(column(field.shape) == 0, 0.0, pltpu.roll(field, 1, 0))


def from_right(field):
    return jnp.where(
        column(field.shape) == COLS - 1, 0.0, pltpu.roll(field, field.shape[0] - 1, 0)
    )


def shifted_transposes(pixels):
    wide = pixels.astype(F32)
    return [
        from_left(wide).astype(BF16).T,
        pixels.T,
        from_right(wide).astype(BF16).T,
    ]


def place(arg):
    return pltpu.SMEM if arg.dtype == jnp.int32 else pltpu.VMEM


def call(kernel, out_shape, flops, nbytes, *args, hbm_in=(), hbm_out=(), scratch=()):
    flat, tree = jax.tree.flatten(out_shape, is_leaf=lambda leaf: hasattr(leaf, "dtype"))
    out_specs = [
        pl.BlockSpec(memory_space=pltpu.HBM if n in hbm_out else pltpu.VMEM)
        for n in range(len(flat))
    ]
    in_specs = [
        pl.BlockSpec(memory_space=pltpu.HBM if n in hbm_in else place(arg))
        for n, arg in enumerate(args)
    ]
    return pl.pallas_call(
        kernel,
        out_shape=out_shape,
        in_specs=in_specs,
        out_specs=jax.tree.unflatten(tree, out_specs),
        scratch_shapes=list(scratch),
        compiler_params=pltpu.CompilerParams(vmem_limit_bytes=VMEM_LIMIT),
        cost_estimate=pl.CostEstimate(flops=flops, bytes_accessed=nbytes, transcendentals=0),
    )(*args)


def shape(dims, dtype):
    return jax.ShapeDtypeStruct(dims, dtype)


def vmem(dims, dtype):
    return pltpu.VMEM(dims, dtype)


def hbm(dims, dtype):
    return pltpu.HBM(dims, dtype)


TAP_FLOPS = 2 * 2 * PIX * C * C


def order_kernel(core, out_ref):
    row = lax.broadcasted_iota(jnp.int32, (C, C), 0)
    col = lax.broadcasted_iota(jnp.int32, (C, C), 1)
    side = (col // 128) ^ core[0]
    source = ((col % 128) // 64) * 128 + ((col % 64) // 4) * 8 + side * 4 + col % 4
    out_ref[...] = jnp.where(row == source, 1.0, 0.0).astype(BF16)


def first_kernel(core, x, g, wt, pm, gh_ref, gp_ref, pair_ref, chip_ref):
    c = core[0]
    for f in range(2):
        pair_ref[f, 0] = x[f, 3 - 3 * c]
        chip_ref[f, 0] = x[f, 3 * c]
        gp_ref[f] = mm(g[f].reshape(PIX, C), pm[...]).astype(BF16)
    g0, g1 = g[0].reshape(PIX, C), g[1].reshape(PIX, C)
    gh_ref[0] = mm_t(g0, wt[2]) + mm_t(g1, wt[1])
    gh_ref[1] = mm_t(g1, wt[2])


def low_high(core, pair, chip):
    first = core[0] == 0
    return jnp.where(first, chip, pair), jnp.where(first, pair, chip)


def own_kernel(x, ws, pre_ref, xt_ref):
    for f in range(2):
        for j in range(3):
            mid = mm(x[f].reshape(PIX, C), ws[3 + j])
            up = mm(x[f, 0:3].reshape(3 * COLS, C), ws[j])
            down = mm(x[f, 1:4].reshape(3 * COLS, C), ws[6 + j])
            zero = jnp.zeros((COLS, C), F32)
            total = (
                mid + jnp.concatenate([zero, up], 0) + jnp.concatenate([down, zero], 0)
            )
            if j == 0:
                acc = from_left(total)
            elif j == 1:
                acc = acc + total
            else:
                acc = acc + from_right(total)
        pre_ref[f] = acc
        for j, t in enumerate(shifted_transposes(x[f].reshape(PIX, C))):
            xt_ref[j, f] = t


def edge_kernel(core, pre, pair, chip, ws, gp, hid_ref, fac_ref, ht_ref, xe_ref, gt_ref):
    for f in range(2):
        low, high = low_high(core, pair[f, 0], chip[f, 0])
        top = from_left(mm(low, ws[0])) + mm(low, ws[1]) + from_right(mm(low, ws[2]))
        end = from_left(mm(high, ws[6])) + mm(high, ws[7]) + from_right(mm(high, ws[8]))
        value = jnp.concatenate(
            [
                pre[f, 0:COLS] + top,
                pre[f, COLS : 3 * COLS],
                pre[f, 3 * COLS :] + end,
            ],
            0,
        )
        sig = jax.nn.sigmoid(value)
        hidden = (value * sig).astype(BF16)
        hid_ref[f] = hidden.reshape(ROWS, COLS, C)
        fac_ref[f] = sig * (1.0 + value * (1.0 - sig))
        ht_ref[f] = hidden.T
        lows, highs = shifted_transposes(low), shifted_transposes(high)
        for j in range(3):
            xe_ref[j, f, 0] = lows[j]
            xe_ref[j, f, 1] = highs[j]
    gt_ref[0] = mm(ht_ref[0], gp[1])
    gt_ref[1] = mm(ht_ref[0], gp[0]) + mm(ht_ref[1], gp[1])


def grad_kernel(
    core, n, gh, fac, xt, xe, ht, gt, wt, pm,
    gpre_hbm, pair_hbm, chip_hbm, keep_ref, send_ref,
    gpre_ref, sems,
):
    def store(tap, value):
        keep_ref[tap] = value[:, : C // 2]
        send_ref[tap] = value[:, C // 2 :].astype(BF16)

    a0, a1 = n[0].reshape(PIX, C), n[1].reshape(PIX, C)
    back0 = gh[0] + mm_t(a0, wt[0])
    back1 = gh[1] + mm_t(a0, wt[1]) + mm_t(a1, wt[0])
    grads = []
    for f, back in enumerate((back0, back1)):
        gpre = (back.astype(BF16).astype(F32) * fac[f]).astype(BF16)
        gpre_ref[f] = gpre.reshape(ROWS, COLS, C)
        grads.append(mm(gpre, pm[...]).astype(BF16))
    c = core[0]
    copies = [
        pltpu.make_async_copy(gpre_ref.at[:, pl.ds(3 - 3 * c, 1)], pair_hbm, sems.at[0]),
        pltpu.make_async_copy(gpre_ref.at[:, pl.ds(3 * c, 1)], chip_hbm, sems.at[1]),
        pltpu.make_async_copy(gpre_ref, gpre_hbm, sems.at[2]),
    ]
    for copy in copies:
        copy.start()
    p0 = mm(a0, pm[...]).astype(BF16)
    p1 = mm(a1, pm[...]).astype(BF16)
    store(9, mm(ht[0], p0) + mm(ht[1], p1))
    store(10, gt[0] + mm(ht[1], p0))
    store(11, gt[1])
    for j in range(3):
        for i in range(3):
            total = None
            for f in range(2):
                own = xt[j, f]
                if i == 0:
                    own = jnp.concatenate([xe[j, f, 0], own[:, : 3 * COLS]], 1)
                elif i == 2:
                    own = jnp.concatenate([own[:, COLS:], xe[j, f, 1]], 1)
                part = mm(own, grads[f])
                total = part if total is None else total + part
            store(3 * i + j, total)
    for copy in copies:
        copy.wait()


def pair_kernel(keep, got, out_ref):
    half = C // 4
    for p in range(TAPS // 2):
        s0 = keep[2 * p] + got[2 * p].astype(F32)
        s1 = keep[2 * p + 1] + got[2 * p + 1].astype(F32)
        low = jnp.concatenate([s0[:, :half], s1[:, :half]], 1).astype(BF16)
        high = jnp.concatenate([s0[:, half:], s1[:, half:]], 1).astype(BF16)
        for a in range(8):
            out_ref[2 * a, :, p * 128 : (p + 1) * 128] = low[32 * a : 32 * a + 32]
            out_ref[2 * a + 1, :, p * 128 : (p + 1) * 128] = high[32 * a : 32 * a + 32]


def plane_kernel(got, out_ref):
    total = got[0].astype(F32)
    for n in range(1, 16):
        total = total + got[n].astype(F32)
    pieces = []
    for p in range(TAPS // 2):
        flipped = total[:, p * 128 : (p + 1) * 128].T
        pieces += [flipped[:64], flipped[64:]]
    wide = jnp.concatenate(pieces, 1)
    for z in range(16):
        out_ref[z] = wide[4 * z : 4 * z + 4]


def last_kernel(got, gs_ref, gt_ref):
    total = got[0]
    for n in range(1, 16):
        total = total + got[n]
    for t in range(9):
        gs_ref[t] = total[:, 32 * t : 32 * t + 32]
    for t in range(3):
        gt_ref[t] = total[:, 32 * (9 + t) : 32 * (9 + t) + 32]


def token_kernel(rows, out_ref):
    out_ref[...] = jnp.zeros(out_ref.shape, F32)


def out_kernel(hid, past, wt, out_ref):
    h0, h1 = hid[0].reshape(PIX, C), hid[1].reshape(PIX, C)
    p0, p1 = past[0].reshape(PIX, C), past[1].reshape(PIX, C)
    first = mm(p0, wt[0]) + mm(p1, wt[1]) + mm(h0, wt[2])
    out_ref[0] = first.astype(BF16).reshape(ROWS, COLS, C)
    second = mm(p1, wt[0]) + mm(h0, wt[1]) + mm(h1, wt[2])
    out_ref[1] = second.astype(BF16).reshape(ROWS, COLS, C)


def back_kernel(core, gpre, pair, chip, ws, token, out_ref):
    for f in range(2):
        low, high = low_high(core, pair[f, 0], chip[f, 0])
        own = gpre[f].reshape(PIX, C)
        after = jnp.concatenate([own[COLS:], high], 0)
        before = jnp.concatenate([low, own[: 3 * COLS]], 0)
        sums = [
            mm_t(after, ws[j]) + mm_t(own, ws[3 + j]) + mm_t(before, ws[6 + j])
            for j in range(3)
        ]
        total = from_right(sums[0]) + sums[1] + from_left(sums[2])
        out_ref[f] = total.astype(BF16).reshape(ROWS, COLS, C)


SPACE = ("xl", "z", "c")


def steps(count):
    forward = [(i, i + 1) for i in range(count - 1)]
    return forward, [(b, a) for a, b in forward]


def to_pair(rows):
    return lax.ppermute(rows, "c", [(0, 1), (1, 0)])


def to_chip(rows):
    across = [(i, i + 1) for i in range(1, 63, 2)]
    return lax.ppermute(rows, SPACE, across + [(b, a) for a, b in across])


def body(frames_in, w_space, w_time, grad_out):
    forward, backward = steps(8)
    core = lax.axis_index("c").reshape(1)
    order = call(order_kernel, shape((C, C), BF16), HINT, 1 << 17, core)
    rows = shape((2, 1, COLS, C), BF16)
    later = lax.ppermute(grad_out, "tm", backward)
    gh_part, gp, pair, chip = call(
        first_kernel,
        (shape((2, PIX, C), F32), shape((2, PIX, C), BF16), rows, rows),
        4 * TAP_FLOPS,
        4 << 20,
        core, frames_in, grad_out, w_time, order,
    )
    pair, chip = to_pair(pair), to_chip(chip)
    pre_part, xt = call(
        own_kernel,
        (shape((2, PIX, C), F32), shape((3, 2, C, PIX), BF16)),
        9 * TAP_FLOPS,
        4 << 20,
        frames_in, w_space,
    )
    hidden, factor, ht, xe, gt_part = call(
        edge_kernel,
        (
            shape((2, ROWS, COLS, C), BF16),
            shape((2, PIX, C), F32),
            shape((2, C, PIX), BF16),
            shape((3, 2, 2, C, COLS), BF16),
            shape((2, C, C), F32),
        ),
        5 * TAP_FLOPS,
        8 << 20,
        core, pre_part, pair, chip, w_space, gp,
    )
    grad_pre, pair, chip, keep, send = call(
        grad_kernel,
        (
            hbm((2, ROWS, COLS, C), BF16),
            hbm((2, 1, COLS, C), BF16),
            hbm((2, 1, COLS, C), BF16),
            vmem((TAPS, C, C // 2), F32),
            vmem((TAPS, C, C // 2), BF16),
        ),
        15 * TAP_FLOPS,
        10 << 20,
        core, later, gh_part, factor, xt, xe, ht, gt_part, w_time, order,
        hbm_out=(0, 1, 2),
        scratch=[pltpu.VMEM((2, ROWS, COLS, C), BF16), pltpu.SemaphoreType.DMA((3,))],
    )
    got = lax.ppermute(send, "c", [(0, 1), (1, 0)])
    chunks = call(pair_kernel, shape((16, 32, 768), BF16), 1 << 20, 4 << 20, keep, got)
    chunks = lax.all_to_all(chunks, ("tm", "xl"), split_axis=0, concat_axis=0, tiled=True)
    pair = to_pair(pair)
    token = call(token_kernel, shape((8, 128), F32), HINT, 1 << 12, pair, hbm_in=(0,))
    chip, token = lax.optimization_barrier((chip, token))
    chip = to_chip(chip)
    hidden, chip = lax.optimization_barrier((hidden, chip))
    past = lax.ppermute(hidden, "tm", forward)
    chunks, pair, chip = lax.optimization_barrier((chunks, pair, chip))
    block_out = call(
        out_kernel,
        shape((2, ROWS, COLS, C), BF16),
        3 * TAP_FLOPS,
        2 << 20,
        hidden, past, w_time,
    )
    grad_in = call(
        back_kernel,
        shape((2, ROWS, COLS, C), BF16),
        9 * TAP_FLOPS,
        4 << 20,
        core, grad_pre, pair, chip, w_space, token,
    )
    rows = call(plane_kernel, shape((16, 4, 384), F32), 1 << 20, 1 << 20, chunks)
    rows = lax.all_to_all(rows, "z", split_axis=0, concat_axis=0, tiled=True)
    rows, block_out = lax.optimization_barrier((rows, block_out))
    grad_space, grad_time = call(
        last_kernel, (shape((9, 4, 32), F32), shape((3, 4, 32), F32)), 1 << 16, 1 << 18, rows
    )
    return (
        block_out,
        grad_in,
        jnp.transpose(grad_space, (0, 2, 1)),
        jnp.transpose(grad_time, (0, 2, 1)),
    )


def solution(mesh):
    fine = Mesh(mesh.devices.reshape(8, 2, 16, 2), ("tm",) + SPACE)
    in_specs = (P("tm", SPACE, None, None), P(), P(), P("tm", SPACE, None, None))
    out_specs = (
        P("tm", SPACE, None, None),
        P("tm", SPACE, None, None),
        P(None, "tm", SPACE),
        P(None, "tm", SPACE),
    )
    return jax.shard_map(body, mesh=fine, in_specs=in_specs, out_specs=out_specs, check_vma=False)
```

```python
import jax
import jax.numpy as jnp
from jax import lax
from jax.experimental import pallas as pl
from jax.experimental.pallas import tpu as pltpu
from jax.sharding import Mesh
from jax.sharding import PartitionSpec as P

F32 = jnp.float32
BF16 = jnp.bfloat16
C = 256
COLS = 128
ROWS = 4
PIX = ROWS * COLS
TAPS = 12
VMEM_LIMIT = 16 * 1024 * 1024
HINT = 1 << 33


def mm(a, b):
    return jnp.dot(a, b, preferred_element_type=F32)


def mm_t(a, b):
    return lax.dot_general(a, b, (((1,), (1,)), ((), ())), preferred_element_type=F32)


def column(shape):
    return lax.broadcasted_iota(jnp.int32, shape, 0) % COLS


def from_left(field):
    return jnp.where(column(field.shape) == 0, 0.0, pltpu.roll(field, 1, 0))


def from_right(field):
    return jnp.where(
        column(field.shape) == COLS - 1, 0.0, pltpu.roll(field, field.shape[0] - 1, 0)
    )


def shifted_transposes(pixels):
    wide = pixels.astype(F32)
    return [
        from_left(wide).astype(BF16).T,
        pixels.T,
        from_right(wide).astype(BF16).T,
    ]


def place(arg):
    return pltpu.SMEM if arg.dtype == jnp.int32 else pltpu.VMEM


def call(kernel, out_shape, flops, nbytes, *args, hbm_in=(), hbm_out=(), scratch=()):
    flat, tree = jax.tree.flatten(out_shape, is_leaf=lambda leaf: hasattr(leaf, "dtype"))
    out_specs = [
        pl.BlockSpec(memory_space=pltpu.HBM if n in hbm_out else pltpu.VMEM)
        for n in range(len(flat))
    ]
    in_specs = [
        pl.BlockSpec(memory_space=pltpu.HBM if n in hbm_in else place(arg))
        for n, arg in enumerate(args)
    ]
    return pl.pallas_call(
        kernel,
        out_shape=out_shape,
        in_specs=in_specs,
        out_specs=jax.tree.unflatten(tree, out_specs),
        scratch_shapes=list(scratch),
        compiler_params=pltpu.CompilerParams(vmem_limit_bytes=VMEM_LIMIT),
        cost_estimate=pl.CostEstimate(flops=flops, bytes_accessed=nbytes, transcendentals=0),
    )(*args)


def shape(dims, dtype):
    return jax.ShapeDtypeStruct(dims, dtype)


def vmem(dims, dtype):
    return pltpu.VMEM(dims, dtype)


def hbm(dims, dtype):
    return pltpu.HBM(dims, dtype)


TAP_FLOPS = 2 * 2 * PIX * C * C


def order_kernel(core, out_ref):
    row = lax.broadcasted_iota(jnp.int32, (C, C), 0)
    col = lax.broadcasted_iota(jnp.int32, (C, C), 1)
    side = (col // 128) ^ core[0]
    source = ((col % 128) // 64) * 128 + ((col % 64) // 4) * 8 + side * 4 + col % 4
    out_ref[...] = jnp.where(row == source, 1.0, 0.0).astype(BF16)


def first_kernel(core, x, g, wt, pm, gh_ref, gp_ref, pair_ref, chip_ref):
    c = core[0]
    for f in range(2):
        pair_ref[f, 0] = x[f, 3 - 3 * c]
        chip_ref[f, 0] = x[f, 3 * c]
        gp_ref[f] = mm(g[f].reshape(PIX, C), pm[...]).astype(BF16)
    g0, g1 = g[0].reshape(PIX, C), g[1].reshape(PIX, C)
    gh_ref[0] = mm_t(g0, wt[2]) + mm_t(g1, wt[1])
    gh_ref[1] = mm_t(g1, wt[2])


def low_high(core, pair, chip):
    first = core[0] == 0
    return jnp.where(first, chip, pair), jnp.where(first, pair, chip)


def own_kernel(x, ws, pre_ref, xt_ref):
    for f in range(2):
        for j in range(3):
            mid = mm(x[f].reshape(PIX, C), ws[3 + j])
            up = mm(x[f, 0:3].reshape(3 * COLS, C), ws[j])
            down = mm(x[f, 1:4].reshape(3 * COLS, C), ws[6 + j])
            zero = jnp.zeros((COLS, C), F32)
            total = (
                mid + jnp.concatenate([zero, up], 0) + jnp.concatenate([down, zero], 0)
            )
            if j == 0:
                acc = from_left(total)
            elif j == 1:
                acc = acc + total
            else:
                acc = acc + from_right(total)
        pre_ref[f] = acc
        for j, t in enumerate(shifted_transposes(x[f].reshape(PIX, C))):
            xt_ref[j, f] = t


def edge_kernel(core, pre, pair, chip, ws, gp, hid_ref, fac_ref, ht_ref, xe_ref, gt_ref):
    for f in range(2):
        low, high = low_high(core, pair[f, 0], chip[f, 0])
        top = from_left(mm(low, ws[0])) + mm(low, ws[1]) + from_right(mm(low, ws[2]))
        end = from_left(mm(high, ws[6])) + mm(high, ws[7]) + from_right(mm(high, ws[8]))
        value = jnp.concatenate(
            [
                pre[f, 0:COLS] + top,
                pre[f, COLS : 3 * COLS],
                pre[f, 3 * COLS :] + end,
            ],
            0,
        )
        sig = jax.nn.sigmoid(value)
        hidden = (value * sig).astype(BF16)
        hid_ref[f] = hidden.reshape(ROWS, COLS, C)
        fac_ref[f] = sig * (1.0 + value * (1.0 - sig))
        ht_ref[f] = hidden.T
        lows, highs = shifted_transposes(low), shifted_transposes(high)
        for j in range(3):
            xe_ref[j, f, 0] = lows[j]
            xe_ref[j, f, 1] = highs[j]
    gt_ref[0] = mm(ht_ref[0], gp[1])
    gt_ref[1] = mm(ht_ref[0], gp[0]) + mm(ht_ref[1], gp[1])


def grad_kernel(
    core, n, gh, fac, xt, xe, ht, gt, wt, pm,
    gpre_hbm, pair_hbm, chip_hbm, keep_ref, send_ref,
    gpre_ref, sems,
):
    def store(tap, value):
        keep_ref[tap] = value[:, : C // 2]
        send_ref[tap] = value[:, C // 2 :].astype(BF16)

    a0, a1 = n[0].reshape(PIX, C), n[1].reshape(PIX, C)
    back0 = gh[0] + mm_t(a0, wt[0])
    back1 = gh[1] + mm_t(a0, wt[1]) + mm_t(a1, wt[0])
    grads = []
    for f, back in enumerate((back0, back1)):
        gpre = (back.astype(BF16).astype(F32) * fac[f]).astype(BF16)
        gpre_ref[f] = gpre.reshape(ROWS, COLS, C)
        grads.append(mm(gpre, pm[...]).astype(BF16))
    c = core[0]
    copies = [
        pltpu.make_async_copy(gpre_ref.at[:, pl.ds(3 - 3 * c, 1)], pair_hbm, sems.at[0]),
        pltpu.make_async_copy(gpre_ref.at[:, pl.ds(3 * c, 1)], chip_hbm, sems.at[1]),
        pltpu.make_async_copy(gpre_ref, gpre_hbm, sems.at[2]),
    ]
    for copy in copies:
        copy.start()
    p0 = mm(a0, pm[...]).astype(BF16)
    p1 = mm(a1, pm[...]).astype(BF16)
    store(9, mm(ht[0], p0) + mm(ht[1], p1))
    store(10, gt[0] + mm(ht[1], p0))
    store(11, gt[1])
    for j in range(3):
        for i in range(3):
            total = None
            for f in range(2):
                own = xt[j, f]
                if i == 0:
                    own = jnp.concatenate([xe[j, f, 0], own[:, : 3 * COLS]], 1)
                elif i == 2:
                    own = jnp.concatenate([own[:, COLS:], xe[j, f, 1]], 1)
                part = mm(own, grads[f])
                total = part if total is None else total + part
            store(3 * i + j, total)
    for copy in copies:
        copy.wait()


def pair_kernel(keep, got, chip, out_hbm, out_ref, sems):
    half = C // 4
    copies = []
    for p in range(TAPS // 2):
        s0 = keep[2 * p] + got[2 * p].astype(F32)
        s1 = keep[2 * p + 1] + got[2 * p + 1].astype(F32)
        low = jnp.concatenate([s0[:, :half], s1[:, :half]], 1).astype(BF16)
        high = jnp.concatenate([s0[:, half:], s1[:, half:]], 1).astype(BF16)
        for a in range(8):
            out_ref[a, 32 * p : 32 * p + 32] = low[32 * a : 32 * a + 32]
            out_ref[8 + a, 32 * p : 32 * p + 32] = high[32 * a : 32 * a + 32]
        if p % 2 == 1:
            part = pl.ds(32 * (p - 1), 64)
            copy = pltpu.make_async_copy(
                out_ref.at[:, part], out_hbm.at[:, part], sems.at[p // 2]
            )
            copy.start()
            copies.append(copy)
    for copy in copies:
        copy.wait()


def plane_kernel(got, pair, chip, out_ref):
    total = got[0].astype(F32)
    for n in range(1, 16):
        total = total + got[n].astype(F32)
    pieces = []
    for p in range(TAPS // 2):
        flipped = total[32 * p : 32 * p + 32].T
        pieces += [flipped[:64], flipped[64:]]
    wide = jnp.concatenate(pieces, 1)
    for z in range(16):
        out_ref[z] = wide[4 * z : 4 * z + 4]


def last_kernel(got, gs_ref, gt_ref):
    total = got[0]
    for n in range(1, 16):
        total = total + got[n]
    for t in range(9):
        gs_ref[t] = total[:, 32 * t : 32 * t + 32]
    for t in range(3):
        gt_ref[t] = total[:, 32 * (9 + t) : 32 * (9 + t) + 32]


def token_kernel(*refs):
    out_ref = refs[-1]
    out_ref[...] = jnp.zeros(out_ref.shape, F32)


def out_kernel(hid, past, wt, out_ref):
    h0, h1 = hid[0].reshape(PIX, C), hid[1].reshape(PIX, C)
    p0, p1 = past[0].reshape(PIX, C), past[1].reshape(PIX, C)
    first = mm(p0, wt[0]) + mm(p1, wt[1]) + mm(h0, wt[2])
    out_ref[0] = first.astype(BF16).reshape(ROWS, COLS, C)
    second = mm(p1, wt[0]) + mm(h0, wt[1]) + mm(h1, wt[2])
    out_ref[1] = second.astype(BF16).reshape(ROWS, COLS, C)


def back_kernel(core, gpre, pair, chip, ws, token, arrived, out_ref):
    for f in range(2):
        low, high = low_high(core, pair[f, 0], chip[f, 0])
        own = gpre[f].reshape(PIX, C)
        after = jnp.concatenate([own[COLS:], high], 0)
        before = jnp.concatenate([low, own[: 3 * COLS]], 0)
        sums = [
            mm_t(after, ws[j]) + mm_t(own, ws[3 + j]) + mm_t(before, ws[6 + j])
            for j in range(3)
        ]
        total = from_right(sums[0]) + sums[1] + from_left(sums[2])
        out_ref[f] = total.astype(BF16).reshape(ROWS, COLS, C)


SPACE = ("xl", "z", "c")


def steps(count):
    forward = [(i, i + 1) for i in range(count - 1)]
    return forward, [(b, a) for a, b in forward]


def to_pair(rows):
    return lax.ppermute(rows, "c", [(0, 1), (1, 0)])


def to_chip(rows):
    across = [(i, i + 1) for i in range(1, 63, 2)]
    return lax.ppermute(rows, SPACE, across + [(b, a) for a, b in across])


def body(frames_in, w_space, w_time, grad_out):
    forward, backward = steps(8)
    core = lax.axis_index("c").reshape(1)
    order = call(order_kernel, shape((C, C), BF16), HINT, 1 << 17, core)
    rows = shape((2, 1, COLS, C), BF16)
    later = lax.ppermute(grad_out, "tm", backward)
    gh_part, gp, pair, chip = call(
        first_kernel,
        (shape((2, PIX, C), F32), shape((2, PIX, C), BF16), rows, rows),
        4 * TAP_FLOPS,
        4 << 20,
        core, frames_in, grad_out, w_time, order,
    )
    pair, chip = to_pair(pair), to_chip(chip)
    pre_part, xt = call(
        own_kernel,
        (shape((2, PIX, C), F32), shape((3, 2, C, PIX), BF16)),
        9 * TAP_FLOPS,
        4 << 20,
        frames_in, w_space,
    )
    hidden, factor, ht, xe, gt_part = call(
        edge_kernel,
        (
            shape((2, ROWS, COLS, C), BF16),
            shape((2, PIX, C), F32),
            shape((2, C, PIX), BF16),
            shape((3, 2, 2, C, COLS), BF16),
            shape((2, C, C), F32),
        ),
        5 * TAP_FLOPS,
        8 << 20,
        core, pre_part, pair, chip, w_space, gp,
    )
    grad_pre, pair, chip, keep, send = call(
        grad_kernel,
        (
            hbm((2, ROWS, COLS, C), BF16),
            hbm((2, 1, COLS, C), BF16),
            vmem((2, 1, COLS, C), BF16),
            vmem((TAPS, C, C // 2), F32),
            vmem((TAPS, C, C // 2), BF16),
        ),
        15 * TAP_FLOPS,
        10 << 20,
        core, later, gh_part, factor, xt, xe, ht, gt_part, w_time, order,
        hbm_out=(0, 1),
        scratch=[pltpu.VMEM((2, ROWS, COLS, C), BF16), pltpu.SemaphoreType.DMA((3,))],
    )
    got = lax.ppermute(send, "c", [(0, 1), (1, 0)])
    chunks = call(
        pair_kernel, hbm((16, 192, 128), BF16), 1 << 20, 4 << 20, keep, got, chip,
        hbm_out=(0,),
        scratch=[pltpu.VMEM((16, 192, 128), BF16), pltpu.SemaphoreType.DMA((3,))],
    )
    chunks = lax.all_to_all(chunks, ("xl", "tm"), split_axis=0, concat_axis=0, tiled=True)
    pair = to_pair(pair)
    token = call(token_kernel, shape((8, 128), F32), HINT, 1 << 12, pair, chip, hbm_in=(0,))
    chip, token = lax.optimization_barrier((chip, token))
    chip = to_chip(chip)
    arrived = call(token_kernel, shape((8, 128), F32), 0, 1 << 12, chip, pair, hbm_in=(0, 1))
    hidden, arrived = lax.optimization_barrier((hidden, arrived))
    past = lax.ppermute(hidden, "tm", forward)
    chunks, arrived = lax.optimization_barrier((chunks, arrived))
    block_out = call(
        out_kernel,
        shape((2, ROWS, COLS, C), BF16),
        3 * TAP_FLOPS,
        2 << 20,
        hidden, past, w_time,
    )
    grad_in = call(
        back_kernel,
        shape((2, ROWS, COLS, C), BF16),
        9 * TAP_FLOPS,
        4 << 20,
        core, grad_pre, pair, chip, w_space, token, arrived,
    )
    rows = call(plane_kernel, shape((16, 4, 384), F32), 1 << 20, 1 << 20, chunks, pair, chip)
    rows = lax.all_to_all(rows, "z", split_axis=0, concat_axis=0, tiled=True)
    rows, block_out = lax.optimization_barrier((rows, block_out))
    grad_space, grad_time = call(
        last_kernel, (shape((9, 4, 32), F32), shape((3, 4, 32), F32)), 1 << 16, 1 << 18, rows
    )
    return (
        block_out,
        grad_in,
        jnp.transpose(grad_space, (0, 2, 1)),
        jnp.transpose(grad_time, (0, 2, 1)),
    )


def solution(mesh):
    fine = Mesh(mesh.devices.reshape(8, 2, 16, 2), ("tm",) + SPACE)
    in_specs = (P("tm", SPACE, None, None), P(), P(), P("tm", SPACE, None, None))
    out_specs = (
        P("tm", SPACE, None, None),
        P("tm", SPACE, None, None),
        P(None, "tm", SPACE),
        P(None, "tm", SPACE),
    )
    return jax.shard_map(body, mesh=fine, in_specs=in_specs, out_specs=out_specs, check_vma=False)
```

```python
import jax
import jax.numpy as jnp
from jax import lax
from jax.experimental import pallas as pl
from jax.experimental.pallas import tpu as pltpu
from jax.sharding import Mesh
from jax.sharding import PartitionSpec as P

F32 = jnp.float32
BF16 = jnp.bfloat16
C = 256
COLS = 128
ROWS = 4
PIX = ROWS * COLS
TAPS = 12
VMEM_LIMIT = 16 * 1024 * 1024
HINT = 1 << 33


def mm(a, b):
    return jnp.dot(a, b, preferred_element_type=F32)


def mm_t(a, b):
    return lax.dot_general(a, b, (((1,), (1,)), ((), ())), preferred_element_type=F32)


def column(shape):
    return lax.broadcasted_iota(jnp.int32, shape, 0) % COLS


def from_left(field):
    return jnp.where(column(field.shape) == 0, 0.0, pltpu.roll(field, 1, 0))


def from_right(field):
    return jnp.where(
        column(field.shape) == COLS - 1, 0.0, pltpu.roll(field, field.shape[0] - 1, 0)
    )


def shifted_transposes(pixels):
    wide = pixels.astype(F32)
    return [
        from_left(wide).astype(BF16).T,
        pixels.T,
        from_right(wide).astype(BF16).T,
    ]


def place(arg):
    return pltpu.SMEM if arg.dtype == jnp.int32 else pltpu.VMEM


def call(kernel, out_shape, flops, nbytes, *args, hbm_in=(), hbm_out=(), scratch=()):
    flat, tree = jax.tree.flatten(out_shape, is_leaf=lambda leaf: hasattr(leaf, "dtype"))
    out_specs = [
        pl.BlockSpec(memory_space=pltpu.HBM if n in hbm_out else pltpu.VMEM)
        for n in range(len(flat))
    ]
    in_specs = [
        pl.BlockSpec(memory_space=pltpu.HBM if n in hbm_in else place(arg))
        for n, arg in enumerate(args)
    ]
    return pl.pallas_call(
        kernel,
        out_shape=out_shape,
        in_specs=in_specs,
        out_specs=jax.tree.unflatten(tree, out_specs),
        scratch_shapes=list(scratch),
        compiler_params=pltpu.CompilerParams(vmem_limit_bytes=VMEM_LIMIT),
        cost_estimate=pl.CostEstimate(flops=flops, bytes_accessed=nbytes, transcendentals=0),
    )(*args)


def shape(dims, dtype):
    return jax.ShapeDtypeStruct(dims, dtype)


def vmem(dims, dtype):
    return pltpu.VMEM(dims, dtype)


def hbm(dims, dtype):
    return pltpu.HBM(dims, dtype)


TAP_FLOPS = 2 * 2 * PIX * C * C


def order_kernel(core, out_ref):
    row = lax.broadcasted_iota(jnp.int32, (C, C), 0)
    col = lax.broadcasted_iota(jnp.int32, (C, C), 1)
    side = (col // 128) ^ core[0]
    source = ((col % 128) // 64) * 128 + ((col % 64) // 4) * 8 + side * 4 + col % 4
    out_ref[...] = jnp.where(row == source, 1.0, 0.0).astype(BF16)


def first_kernel(core, x, g, wt, pm, gh_ref, gp_ref, pair_ref, chip_ref):
    c = core[0]
    for f in range(2):
        pair_ref[f, 0] = x[f, 3 - 3 * c]
        chip_ref[f, 0] = x[f, 3 * c]
        gp_ref[f] = mm(g[f].reshape(PIX, C), pm[...]).astype(BF16)
    g0, g1 = g[0].reshape(PIX, C), g[1].reshape(PIX, C)
    gh_ref[0] = mm_t(g0, wt[2]) + mm_t(g1, wt[1])
    gh_ref[1] = mm_t(g1, wt[2])


def low_high(core, pair, chip):
    first = core[0] == 0
    return jnp.where(first, chip, pair), jnp.where(first, pair, chip)


def own_kernel(x, ws, pre_ref, xt_ref):
    for f in range(2):
        for j in range(3):
            mid = mm(x[f].reshape(PIX, C), ws[3 + j])
            up = mm(x[f, 0:3].reshape(3 * COLS, C), ws[j])
            down = mm(x[f, 1:4].reshape(3 * COLS, C), ws[6 + j])
            zero = jnp.zeros((COLS, C), F32)
            total = (
                mid + jnp.concatenate([zero, up], 0) + jnp.concatenate([down, zero], 0)
            )
            if j == 0:
                acc = from_left(total)
            elif j == 1:
                acc = acc + total
            else:
                acc = acc + from_right(total)
        pre_ref[f] = acc
        for j, t in enumerate(shifted_transposes(x[f].reshape(PIX, C))):
            xt_ref[j, f] = t


def edge_kernel(core, pre, pair, chip, ws, gp, hid_ref, fac_ref, ht_ref, xe_ref, gt_ref):
    for f in range(2):
        low, high = low_high(core, pair[f, 0], chip[f, 0])
        top = from_left(mm(low, ws[0])) + mm(low, ws[1]) + from_right(mm(low, ws[2]))
        end = from_left(mm(high, ws[6])) + mm(high, ws[7]) + from_right(mm(high, ws[8]))
        value = jnp.concatenate(
            [
                pre[f, 0:COLS] + top,
                pre[f, COLS : 3 * COLS],
                pre[f, 3 * COLS :] + end,
            ],
            0,
        )
        sig = jax.nn.sigmoid(value)
        hidden = (value * sig).astype(BF16)
        hid_ref[f] = hidden.reshape(ROWS, COLS, C)
        fac_ref[f] = sig * (1.0 + value * (1.0 - sig))
        ht_ref[f] = hidden.T
        lows, highs = shifted_transposes(low), shifted_transposes(high)
        for j in range(3):
            xe_ref[j, f, 0] = lows[j]
            xe_ref[j, f, 1] = highs[j]
    gt_ref[0] = mm(ht_ref[0], gp[1])
    gt_ref[1] = mm(ht_ref[0], gp[0]) + mm(ht_ref[1], gp[1])


def grad_kernel(
    core, n, gh, fac, xt, xe, ht, gt, wt, pm,
    gpre_hbm, pair_hbm, keep_ref, send_ref,
    gpre_ref, sems,
):
    def store(tap, value):
        keep_ref[tap] = value[:, : C // 2]
        send_ref[tap] = value[:, C // 2 :].astype(BF16)

    a0, a1 = n[0].reshape(PIX, C), n[1].reshape(PIX, C)
    back0 = gh[0] + mm_t(a0, wt[0])
    back1 = gh[1] + mm_t(a0, wt[1]) + mm_t(a1, wt[0])
    grads = []
    for f, back in enumerate((back0, back1)):
        gpre = (back.astype(BF16).astype(F32) * fac[f]).astype(BF16)
        gpre_ref[f] = gpre.reshape(ROWS, COLS, C)
        grads.append(mm(gpre, pm[...]).astype(BF16))
    c = core[0]
    copies = [
        pltpu.make_async_copy(gpre_ref.at[:, pl.ds(3 - 3 * c, 1)], pair_hbm, sems.at[0]),
        pltpu.make_async_copy(gpre_ref, gpre_hbm, sems.at[1]),
    ]
    for copy in copies:
        copy.start()
    p0 = mm(a0, pm[...]).astype(BF16)
    p1 = mm(a1, pm[...]).astype(BF16)
    store(9, mm(ht[0], p0) + mm(ht[1], p1))
    store(10, gt[0] + mm(ht[1], p0))
    store(11, gt[1])
    for j in range(3):
        for i in range(3):
            total = None
            for f in range(2):
                own = xt[j, f]
                if i == 0:
                    own = jnp.concatenate([xe[j, f, 0], own[:, : 3 * COLS]], 1)
                elif i == 2:
                    own = jnp.concatenate([own[:, COLS:], xe[j, f, 1]], 1)
                part = mm(own, grads[f])
                total = part if total is None else total + part
            store(3 * i + j, total)
    for copy in copies:
        copy.wait()


def pair_kernel(core, keep, got, gpre, out_hbm, chip_ref, out_ref, sems):
    half = C // 4
    rows = gpre.at[:, pl.ds(3 * core[0], 1)]
    copies = [pltpu.make_async_copy(rows, chip_ref, sems.at[3])]
    copies[0].start()
    for p in range(TAPS // 2):
        s0 = keep[2 * p] + got[2 * p].astype(F32)
        s1 = keep[2 * p + 1] + got[2 * p + 1].astype(F32)
        low = jnp.concatenate([s0[:, :half], s1[:, :half]], 1).astype(BF16)
        high = jnp.concatenate([s0[:, half:], s1[:, half:]], 1).astype(BF16)
        for a in range(8):
            out_ref[a, 32 * p : 32 * p + 32] = low[32 * a : 32 * a + 32]
            out_ref[8 + a, 32 * p : 32 * p + 32] = high[32 * a : 32 * a + 32]
        if p % 2 == 1:
            part = pl.ds(32 * (p - 1), 64)
            copy = pltpu.make_async_copy(
                out_ref.at[:, part], out_hbm.at[:, part], sems.at[p // 2]
            )
            copy.start()
            copies.append(copy)
    for copy in copies:
        copy.wait()


def plane_kernel(got, pair, chip, out_ref):
    total = got[0].astype(F32)
    for n in range(1, 16):
        total = total + got[n].astype(F32)
    pieces = []
    for p in range(TAPS // 2):
        flipped = total[32 * p : 32 * p + 32].T
        pieces += [flipped[:64], flipped[64:]]
    wide = jnp.concatenate(pieces, 1)
    for z in range(16):
        out_ref[z] = wide[4 * z : 4 * z + 4]


def last_kernel(got, gs_ref, gt_ref):
    total = got[0]
    for n in range(1, 16):
        total = total + got[n]
    for t in range(9):
        gs_ref[t] = total[:, 32 * t : 32 * t + 32]
    for t in range(3):
        gt_ref[t] = total[:, 32 * (9 + t) : 32 * (9 + t) + 32]


def token_kernel(*refs):
    out_ref = refs[-1]
    out_ref[...] = jnp.zeros(out_ref.shape, F32)


def out_kernel(hid, past, wt, out_ref):
    h0, h1 = hid[0].reshape(PIX, C), hid[1].reshape(PIX, C)
    p0, p1 = past[0].reshape(PIX, C), past[1].reshape(PIX, C)
    first = mm(p0, wt[0]) + mm(p1, wt[1]) + mm(h0, wt[2])
    out_ref[0] = first.astype(BF16).reshape(ROWS, COLS, C)
    second = mm(p1, wt[0]) + mm(h0, wt[1]) + mm(h1, wt[2])
    out_ref[1] = second.astype(BF16).reshape(ROWS, COLS, C)


def back_kernel(core, gpre, pair, chip, ws, token, arrived, out_ref):
    for f in range(2):
        low, high = low_high(core, pair[f, 0], chip[f, 0])
        own = gpre[f].reshape(PIX, C)
        after = jnp.concatenate([own[COLS:], high], 0)
        before = jnp.concatenate([low, own[: 3 * COLS]], 0)
        sums = [
            mm_t(after, ws[j]) + mm_t(own, ws[3 + j]) + mm_t(before, ws[6 + j])
            for j in range(3)
        ]
        total = from_right(sums[0]) + sums[1] + from_left(sums[2])
        out_ref[f] = total.astype(BF16).reshape(ROWS, COLS, C)


SPACE = ("xl", "z", "c")


def steps(count):
    forward = [(i, i + 1) for i in range(count - 1)]
    return forward, [(b, a) for a, b in forward]


def to_pair(rows):
    return lax.ppermute(rows, "c", [(0, 1), (1, 0)])


def to_chip(rows):
    across = [(i, i + 1) for i in range(1, 63, 2)]
    return lax.ppermute(rows, SPACE, across + [(b, a) for a, b in across])


def body(frames_in, w_space, w_time, grad_out):
    forward, backward = steps(8)
    core = lax.axis_index("c").reshape(1)
    order = call(order_kernel, shape((C, C), BF16), HINT, 1 << 17, core)
    rows = shape((2, 1, COLS, C), BF16)
    later = lax.ppermute(grad_out, "tm", backward)
    gh_part, gp, pair, chip = call(
        first_kernel,
        (shape((2, PIX, C), F32), shape((2, PIX, C), BF16), rows, rows),
        4 * TAP_FLOPS,
        4 << 20,
        core, frames_in, grad_out, w_time, order,
    )
    pair, chip = to_pair(pair), to_chip(chip)
    pre_part, xt = call(
        own_kernel,
        (shape((2, PIX, C), F32), shape((3, 2, C, PIX), BF16)),
        9 * TAP_FLOPS,
        4 << 20,
        frames_in, w_space,
    )
    hidden, factor, ht, xe, gt_part = call(
        edge_kernel,
        (
            shape((2, ROWS, COLS, C), BF16),
            shape((2, PIX, C), F32),
            shape((2, C, PIX), BF16),
            shape((3, 2, 2, C, COLS), BF16),
            shape((2, C, C), F32),
        ),
        5 * TAP_FLOPS,
        8 << 20,
        core, pre_part, pair, chip, w_space, gp,
    )
    grad_pre, pair, keep, send = call(
        grad_kernel,
        (
            hbm((2, ROWS, COLS, C), BF16),
            hbm((2, 1, COLS, C), BF16),
            vmem((TAPS, C, C // 2), F32),
            vmem((TAPS, C, C // 2), BF16),
        ),
        15 * TAP_FLOPS,
        10 << 20,
        core, later, gh_part, factor, xt, xe, ht, gt_part, w_time, order,
        hbm_out=(0, 1),
        scratch=[pltpu.VMEM((2, ROWS, COLS, C), BF16), pltpu.SemaphoreType.DMA((2,))],
    )
    got = lax.ppermute(send, "c", [(0, 1), (1, 0)])
    chunks, chip = call(
        pair_kernel,
        (hbm((16, 192, 128), BF16), vmem((2, 1, COLS, C), BF16)),
        1 << 20,
        4 << 20,
        core, keep, got, pltpu.with_memory_space_constraint(grad_pre, pltpu.HBM),
        hbm_in=(3,),
        hbm_out=(0,),
        scratch=[pltpu.VMEM((16, 192, 128), BF16), pltpu.SemaphoreType.DMA((4,))],
    )
    chunks = lax.all_to_all(chunks, ("xl", "tm"), split_axis=0, concat_axis=0, tiled=True)
    pair = to_pair(pair)
    token = call(token_kernel, shape((8, 128), F32), HINT, 1 << 12, pair, chip, hbm_in=(0,))
    chip, token = lax.optimization_barrier((chip, token))
    chip = to_chip(chip)
    arrived = call(token_kernel, shape((8, 128), F32), 0, 1 << 12, chip, pair, hbm_in=(0, 1))
    hidden, arrived = lax.optimization_barrier((hidden, arrived))
    past = lax.ppermute(hidden, "tm", forward)
    chunks, arrived = lax.optimization_barrier((chunks, arrived))
    block_out = call(
        out_kernel,
        shape((2, ROWS, COLS, C), BF16),
        3 * TAP_FLOPS,
        2 << 20,
        hidden, past, w_time,
    )
    grad_in = call(
        back_kernel,
        shape((2, ROWS, COLS, C), BF16),
        9 * TAP_FLOPS,
        4 << 20,
        core, grad_pre, pair, chip, w_space, token, arrived,
    )
    rows = call(plane_kernel, shape((16, 4, 384), F32), 1 << 20, 1 << 20, chunks, pair, chip)
    rows = lax.all_to_all(rows, "z", split_axis=0, concat_axis=0, tiled=True)
    rows, block_out = lax.optimization_barrier((rows, block_out))
    grad_space, grad_time = call(
        last_kernel, (shape((9, 4, 32), F32), shape((3, 4, 32), F32)), 1 << 16, 1 << 18, rows
    )
    return (
        block_out,
        grad_in,
        jnp.transpose(grad_space, (0, 2, 1)),
        jnp.transpose(grad_time, (0, 2, 1)),
    )


def solution(mesh):
    fine = Mesh(mesh.devices.reshape(8, 2, 16, 2), ("tm",) + SPACE)
    in_specs = (P("tm", SPACE, None, None), P(), P(), P("tm", SPACE, None, None))
    out_specs = (
        P("tm", SPACE, None, None),
        P("tm", SPACE, None, None),
        P(None, "tm", SPACE),
        P(None, "tm", SPACE),
    )
    return jax.shard_map(body, mesh=fine, in_specs=in_specs, out_specs=out_specs, check_vma=False)
```

```python
import jax
import jax.numpy as jnp
from jax import lax
from jax.experimental import pallas as pl
from jax.experimental.pallas import tpu as pltpu
from jax.sharding import Mesh
from jax.sharding import PartitionSpec as P

F32 = jnp.float32
BF16 = jnp.bfloat16
C = 256
COLS = 128
ROWS = 4
PIX = ROWS * COLS
TAPS = 12
VMEM_LIMIT = 16 * 1024 * 1024
HINT = 1 << 33


def mm(a, b):
    return jnp.dot(a, b, preferred_element_type=F32)


def mm_t(a, b):
    return lax.dot_general(a, b, (((1,), (1,)), ((), ())), preferred_element_type=F32)


def column(shape):
    return lax.broadcasted_iota(jnp.int32, shape, 0) % COLS


def from_left(field):
    return jnp.where(column(field.shape) == 0, 0.0, pltpu.roll(field, 1, 0))


def from_right(field):
    return jnp.where(
        column(field.shape) == COLS - 1, 0.0, pltpu.roll(field, field.shape[0] - 1, 0)
    )


def shifted_transposes(pixels):
    wide = pixels.astype(F32)
    return [
        from_left(wide).astype(BF16).T,
        pixels.T,
        from_right(wide).astype(BF16).T,
    ]


def place(arg):
    return pltpu.SMEM if arg.dtype == jnp.int32 else pltpu.VMEM


def call(kernel, out_shape, flops, nbytes, *args, hbm_in=(), hbm_out=(), scratch=()):
    flat, tree = jax.tree.flatten(out_shape, is_leaf=lambda leaf: hasattr(leaf, "dtype"))
    out_specs = [
        pl.BlockSpec(memory_space=pltpu.HBM if n in hbm_out else pltpu.VMEM)
        for n in range(len(flat))
    ]
    in_specs = [
        pl.BlockSpec(memory_space=pltpu.HBM if n in hbm_in else place(arg))
        for n, arg in enumerate(args)
    ]
    return pl.pallas_call(
        kernel,
        out_shape=out_shape,
        in_specs=in_specs,
        out_specs=jax.tree.unflatten(tree, out_specs),
        scratch_shapes=list(scratch),
        compiler_params=pltpu.CompilerParams(vmem_limit_bytes=VMEM_LIMIT),
        cost_estimate=pl.CostEstimate(flops=flops, bytes_accessed=nbytes, transcendentals=0),
    )(*args)


def shape(dims, dtype):
    return jax.ShapeDtypeStruct(dims, dtype)


def vmem(dims, dtype):
    return pltpu.VMEM(dims, dtype)


def hbm(dims, dtype):
    return pltpu.HBM(dims, dtype)


TAP_FLOPS = 2 * 2 * PIX * C * C


def order_kernel(core, out_ref):
    row = lax.broadcasted_iota(jnp.int32, (C, C), 0)
    col = lax.broadcasted_iota(jnp.int32, (C, C), 1)
    side = (col // 128) ^ core[0]
    source = ((col % 128) // 64) * 128 + ((col % 64) // 4) * 8 + side * 4 + col % 4
    out_ref[...] = jnp.where(row == source, 1.0, 0.0).astype(BF16)


def first_kernel(core, x, g, wt, pm, gh_ref, gp_ref, pair_ref, chip_ref):
    c = core[0]
    for f in range(2):
        pair_ref[f, 0] = x[f, 3 - 3 * c]
        chip_ref[f, 0] = x[f, 3 * c]
        gp_ref[f] = mm(g[f].reshape(PIX, C), pm[...]).astype(BF16)
    g0, g1 = g[0].reshape(PIX, C), g[1].reshape(PIX, C)
    gh_ref[0] = mm_t(g0, wt[2]) + mm_t(g1, wt[1])
    gh_ref[1] = mm_t(g1, wt[2])


def low_high(core, pair, chip):
    first = core[0] == 0
    return jnp.where(first, chip, pair), jnp.where(first, pair, chip)


def own_kernel(x, ws, pre_ref, xt_ref):
    for f in range(2):
        for j in range(3):
            mid = mm(x[f].reshape(PIX, C), ws[3 + j])
            up = mm(x[f, 0:3].reshape(3 * COLS, C), ws[j])
            down = mm(x[f, 1:4].reshape(3 * COLS, C), ws[6 + j])
            zero = jnp.zeros((COLS, C), F32)
            total = (
                mid + jnp.concatenate([zero, up], 0) + jnp.concatenate([down, zero], 0)
            )
            if j == 0:
                acc = from_left(total)
            elif j == 1:
                acc = acc + total
            else:
                acc = acc + from_right(total)
        pre_ref[f] = acc
        for j, t in enumerate(shifted_transposes(x[f].reshape(PIX, C))):
            xt_ref[j, f] = t


def edge_kernel(core, pre, pair, chip, ws, gp, hid_ref, fac_ref, ht_ref, xe_ref, gt_ref):
    for f in range(2):
        low, high = low_high(core, pair[f, 0], chip[f, 0])
        top = from_left(mm(low, ws[0])) + mm(low, ws[1]) + from_right(mm(low, ws[2]))
        end = from_left(mm(high, ws[6])) + mm(high, ws[7]) + from_right(mm(high, ws[8]))
        value = jnp.concatenate(
            [
                pre[f, 0:COLS] + top,
                pre[f, COLS : 3 * COLS],
                pre[f, 3 * COLS :] + end,
            ],
            0,
        )
        sig = jax.nn.sigmoid(value)
        hidden = (value * sig).astype(BF16)
        hid_ref[f] = hidden.reshape(ROWS, COLS, C)
        fac_ref[f] = sig * (1.0 + value * (1.0 - sig))
        ht_ref[f] = hidden.T
        lows, highs = shifted_transposes(low), shifted_transposes(high)
        for j in range(3):
            xe_ref[j, f, 0] = lows[j]
            xe_ref[j, f, 1] = highs[j]
    gt_ref[0] = mm(ht_ref[0], gp[1])
    gt_ref[1] = mm(ht_ref[0], gp[0]) + mm(ht_ref[1], gp[1])


def grad_kernel(
    core, n, gh, fac, xt, xe, ht, gt, wt, pm,
    gpre_hbm, pair_hbm, keep_ref, send_ref,
    gpre_ref, sems,
):
    def store(tap, value):
        keep_ref[tap] = value[:, : C // 2]
        send_ref[tap] = value[:, C // 2 :].astype(BF16)

    a0, a1 = n[0].reshape(PIX, C), n[1].reshape(PIX, C)
    back0 = gh[0] + mm_t(a0, wt[0])
    back1 = gh[1] + mm_t(a0, wt[1]) + mm_t(a1, wt[0])
    grads = []
    for f, back in enumerate((back0, back1)):
        gpre = (back.astype(BF16).astype(F32) * fac[f]).astype(BF16)
        gpre_ref[f] = gpre.reshape(ROWS, COLS, C)
        grads.append(mm(gpre, pm[...]).astype(BF16))
    c = core[0]
    copies = [
        pltpu.make_async_copy(gpre_ref.at[:, pl.ds(3 - 3 * c, 1)], pair_hbm, sems.at[0]),
        pltpu.make_async_copy(gpre_ref, gpre_hbm, sems.at[1]),
    ]
    for copy in copies:
        copy.start()
    p0 = mm(a0, pm[...]).astype(BF16)
    p1 = mm(a1, pm[...]).astype(BF16)
    store(9, mm(ht[0], p0) + mm(ht[1], p1))
    store(10, gt[0] + mm(ht[1], p0))
    store(11, gt[1])
    for j in range(3):
        for i in range(3):
            total = None
            for f in range(2):
                own = xt[j, f]
                if i == 0:
                    own = jnp.concatenate([xe[j, f, 0], own[:, : 3 * COLS]], 1)
                elif i == 2:
                    own = jnp.concatenate([own[:, COLS:], xe[j, f, 1]], 1)
                part = mm(own, grads[f])
                total = part if total is None else total + part
            store(3 * i + j, total)
    for copy in copies:
        copy.wait()


def pair_kernel(core, keep, got, gpre, out_hbm, chip_ref, out_ref, sems):
    half = C // 4
    rows = gpre.at[:, pl.ds(3 * core[0], 1)]
    copies = [pltpu.make_async_copy(rows, chip_ref, sems.at[6])]
    copies[0].start()
    for p in range(TAPS // 2):
        s0 = keep[2 * p] + got[2 * p].astype(F32)
        s1 = keep[2 * p + 1] + got[2 * p + 1].astype(F32)
        low = jnp.concatenate([s0[:, :half], s1[:, :half]], 1).astype(BF16)
        high = jnp.concatenate([s0[:, half:], s1[:, half:]], 1).astype(BF16)
        for a in range(8):
            out_ref[a, 32 * p : 32 * p + 32] = low[32 * a : 32 * a + 32]
            out_ref[8 + a, 32 * p : 32 * p + 32] = high[32 * a : 32 * a + 32]
        part = pl.ds(32 * p, 32)
        copy = pltpu.make_async_copy(out_ref.at[:, part], out_hbm.at[:, part], sems.at[p])
        copy.start()
        copies.append(copy)
    for copy in copies:
        copy.wait()


def plane_kernel(got, pair, chip, out_ref):
    parts = [got[n].astype(F32) for n in range(16)]
    while len(parts) > 1:
        parts = [parts[n] + parts[n + 1] for n in range(0, len(parts), 2)]
    four, two = parts[0][:128].T, parts[0][128:].T
    wide = jnp.concatenate([four[:64], two[:64], four[64:], two[64:]], 1)
    for z in range(16):
        out_ref[z] = wide[4 * z : 4 * z + 4]


def last_kernel(got, gs_ref, gt_ref):
    total = got[0]
    for n in range(1, 16):
        total = total + got[n]
    for t in range(TAPS):
        at = 32 * (6 * (t % 2) + t // 2)
        if t < 9:
            gs_ref[t] = total[:, at : at + 32]
        else:
            gt_ref[t - 9] = total[:, at : at + 32]


def token_kernel(*refs):
    out_ref = refs[-1]
    out_ref[...] = jnp.zeros(out_ref.shape, F32)


def out_kernel(hid, past, wt, out_ref):
    h0, h1 = hid[0].reshape(PIX, C), hid[1].reshape(PIX, C)
    p0, p1 = past[0].reshape(PIX, C), past[1].reshape(PIX, C)
    first = mm(p0, wt[0]) + mm(p1, wt[1]) + mm(h0, wt[2])
    out_ref[0] = first.astype(BF16).reshape(ROWS, COLS, C)
    second = mm(p1, wt[0]) + mm(h0, wt[1]) + mm(h1, wt[2])
    out_ref[1] = second.astype(BF16).reshape(ROWS, COLS, C)


def back_kernel(core, gpre, pair, chip, ws, token, arrived, out_ref):
    for f in range(2):
        low, high = low_high(core, pair[f, 0], chip[f, 0])
        own = gpre[f].reshape(PIX, C)
        after = jnp.concatenate([own[COLS:], high], 0)
        before = jnp.concatenate([low, own[: 3 * COLS]], 0)
        sums = [
            mm_t(after, ws[j]) + mm_t(own, ws[3 + j]) + mm_t(before, ws[6 + j])
            for j in range(3)
        ]
        total = from_right(sums[0]) + sums[1] + from_left(sums[2])
        out_ref[f] = total.astype(BF16).reshape(ROWS, COLS, C)


SPACE = ("xl", "z", "c")


def steps(count):
    forward = [(i, i + 1) for i in range(count - 1)]
    return forward, [(b, a) for a, b in forward]


def to_pair(rows):
    return lax.ppermute(rows, "c", [(0, 1), (1, 0)])


def to_chip(rows):
    across = [(i, i + 1) for i in range(1, 63, 2)]
    return lax.ppermute(rows, SPACE, across + [(b, a) for a, b in across])


def body(frames_in, w_space, w_time, grad_out):
    forward, backward = steps(8)
    core = lax.axis_index("c").reshape(1)
    order = call(order_kernel, shape((C, C), BF16), HINT, 1 << 17, core)
    rows = shape((2, 1, COLS, C), BF16)
    later = lax.ppermute(grad_out, "tm", backward)
    gh_part, gp, pair, chip = call(
        first_kernel,
        (shape((2, PIX, C), F32), shape((2, PIX, C), BF16), rows, rows),
        4 * TAP_FLOPS,
        4 << 20,
        core, frames_in, grad_out, w_time, order,
    )
    pair, chip = to_pair(pair), to_chip(chip)
    pre_part, xt = call(
        own_kernel,
        (shape((2, PIX, C), F32), shape((3, 2, C, PIX), BF16)),
        9 * TAP_FLOPS,
        4 << 20,
        frames_in, w_space,
    )
    hidden, factor, ht, xe, gt_part = call(
        edge_kernel,
        (
            shape((2, ROWS, COLS, C), BF16),
            shape((2, PIX, C), F32),
            shape((2, C, PIX), BF16),
            shape((3, 2, 2, C, COLS), BF16),
            shape((2, C, C), F32),
        ),
        5 * TAP_FLOPS,
        8 << 20,
        core, pre_part, pair, chip, w_space, gp,
    )
    grad_pre, pair, keep, send = call(
        grad_kernel,
        (
            hbm((2, ROWS, COLS, C), BF16),
            hbm((2, 1, COLS, C), BF16),
            vmem((TAPS, C, C // 2), F32),
            vmem((TAPS, C, C // 2), BF16),
        ),
        15 * TAP_FLOPS,
        10 << 20,
        core, later, gh_part, factor, xt, xe, ht, gt_part, w_time, order,
        hbm_out=(0, 1),
        scratch=[pltpu.VMEM((2, ROWS, COLS, C), BF16), pltpu.SemaphoreType.DMA((2,))],
    )
    got = lax.ppermute(send, "c", [(0, 1), (1, 0)])
    chunks, chip = call(
        pair_kernel,
        (hbm((16, 192, 128), BF16), vmem((2, 1, COLS, C), BF16)),
        1 << 20,
        4 << 20,
        core, keep, got, pltpu.with_memory_space_constraint(grad_pre, pltpu.HBM),
        hbm_in=(3,),
        hbm_out=(0,),
        scratch=[pltpu.VMEM((16, 192, 128), BF16), pltpu.SemaphoreType.DMA((7,))],
    )
    chunks = lax.all_to_all(chunks, ("xl", "tm"), split_axis=0, concat_axis=0, tiled=True)
    pair = to_pair(pair)
    token = call(token_kernel, shape((8, 128), F32), HINT, 1 << 12, pair, chip, hbm_in=(0,))
    chip, token = lax.optimization_barrier((chip, token))
    chip = to_chip(chip)
    arrived = call(token_kernel, shape((8, 128), F32), 0, 1 << 12, chip, pair, hbm_in=(0, 1))
    hidden, arrived = lax.optimization_barrier((hidden, arrived))
    past = lax.ppermute(hidden, "tm", forward)
    chunks, arrived = lax.optimization_barrier((chunks, arrived))
    block_out = call(
        out_kernel,
        shape((2, ROWS, COLS, C), BF16),
        3 * TAP_FLOPS,
        2 << 20,
        hidden, past, w_time,
    )
    grad_in = call(
        back_kernel,
        shape((2, ROWS, COLS, C), BF16),
        9 * TAP_FLOPS,
        4 << 20,
        core, grad_pre, pair, chip, w_space, token, arrived,
    )
    rows = call(plane_kernel, shape((16, 4, 384), F32), 1 << 20, 1 << 20, chunks, pair, chip)
    rows = lax.all_to_all(rows, "z", split_axis=0, concat_axis=0, tiled=True)
    rows, block_out = lax.optimization_barrier((rows, block_out))
    grad_space, grad_time = call(
        last_kernel, (shape((9, 4, 32), F32), shape((3, 4, 32), F32)), 1 << 16, 1 << 18, rows
    )
    return (
        block_out,
        grad_in,
        jnp.transpose(grad_space, (0, 2, 1)),
        jnp.transpose(grad_time, (0, 2, 1)),
    )


def solution(mesh):
    fine = Mesh(mesh.devices.reshape(8, 2, 16, 2), ("tm",) + SPACE)
    in_specs = (P("tm", SPACE, None, None), P(), P(), P("tm", SPACE, None, None))
    out_specs = (
        P("tm", SPACE, None, None),
        P("tm", SPACE, None, None),
        P(None, "tm", SPACE),
        P(None, "tm", SPACE),
    )
    return jax.shard_map(body, mesh=fine, in_specs=in_specs, out_specs=out_specs, check_vma=False)
```

```python
import jax
import jax.numpy as jnp
from jax import lax
from jax.experimental import pallas as pl
from jax.experimental.pallas import tpu as pltpu
from jax.sharding import Mesh
from jax.sharding import PartitionSpec as P

F32 = jnp.float32
BF16 = jnp.bfloat16
C = 256
COLS = 128
ROWS = 4
PIX = ROWS * COLS
TAPS = 12
VMEM_LIMIT = 16 * 1024 * 1024
HINT = 1 << 33


def mm(a, b):
    return jnp.dot(a, b, preferred_element_type=F32)


def mm_t(a, b):
    return lax.dot_general(a, b, (((1,), (1,)), ((), ())), preferred_element_type=F32)


def column(shape):
    return lax.broadcasted_iota(jnp.int32, shape, 0) % COLS


def from_left(field):
    return jnp.where(column(field.shape) == 0, 0.0, pltpu.roll(field, 1, 0))


def from_right(field):
    return jnp.where(
        column(field.shape) == COLS - 1, 0.0, pltpu.roll(field, field.shape[0] - 1, 0)
    )


def shifted_transposes(pixels):
    wide = pixels.astype(F32)
    return [
        from_left(wide).astype(BF16).T,
        pixels.T,
        from_right(wide).astype(BF16).T,
    ]


def place(arg):
    return pltpu.SMEM if arg.dtype == jnp.int32 else pltpu.VMEM


def call(kernel, out_shape, flops, nbytes, *args, hbm_in=(), hbm_out=(), scratch=()):
    flat, tree = jax.tree.flatten(out_shape, is_leaf=lambda leaf: hasattr(leaf, "dtype"))
    out_specs = [
        pl.BlockSpec(memory_space=pltpu.HBM if n in hbm_out else pltpu.VMEM)
        for n in range(len(flat))
    ]
    in_specs = [
        pl.BlockSpec(memory_space=pltpu.HBM if n in hbm_in else place(arg))
        for n, arg in enumerate(args)
    ]
    return pl.pallas_call(
        kernel,
        out_shape=out_shape,
        in_specs=in_specs,
        out_specs=jax.tree.unflatten(tree, out_specs),
        scratch_shapes=list(scratch),
        compiler_params=pltpu.CompilerParams(vmem_limit_bytes=VMEM_LIMIT),
        cost_estimate=pl.CostEstimate(flops=flops, bytes_accessed=nbytes, transcendentals=0),
    )(*args)


def shape(dims, dtype):
    return jax.ShapeDtypeStruct(dims, dtype)


def vmem(dims, dtype):
    return pltpu.VMEM(dims, dtype)


def hbm(dims, dtype):
    return pltpu.HBM(dims, dtype)


TAP_FLOPS = 2 * 2 * PIX * C * C


def order_kernel(core, out_ref):
    row = lax.broadcasted_iota(jnp.int32, (C, C), 0)
    col = lax.broadcasted_iota(jnp.int32, (C, C), 1)
    side = (col // 128) ^ core[0]
    source = ((col % 128) // 64) * 128 + ((col % 64) // 4) * 8 + side * 4 + col % 4
    out_ref[...] = jnp.where(row == source, 1.0, 0.0).astype(BF16)


def first_kernel(core, x, g, wt, pm, gh_ref, gp_ref, pair_ref, chip_ref):
    c = core[0]
    for f in range(2):
        pair_ref[f, 0] = x[f, 3 - 3 * c]
        chip_ref[f, 0] = x[f, 3 * c]
        gp_ref[f] = mm(g[f].reshape(PIX, C), pm[...]).astype(BF16)
    g0, g1 = g[0].reshape(PIX, C), g[1].reshape(PIX, C)
    gh_ref[0] = mm_t(g0, wt[2]) + mm_t(g1, wt[1])
    gh_ref[1] = mm_t(g1, wt[2])


def low_high(core, pair, chip):
    first = core[0] == 0
    return jnp.where(first, chip, pair), jnp.where(first, pair, chip)


def own_kernel(x, ws, pre_ref, xt_ref):
    for f in range(2):
        for j in range(3):
            mid = mm(x[f].reshape(PIX, C), ws[3 + j])
            up = mm(x[f, 0:3].reshape(3 * COLS, C), ws[j])
            down = mm(x[f, 1:4].reshape(3 * COLS, C), ws[6 + j])
            zero = jnp.zeros((COLS, C), F32)
            total = (
                mid + jnp.concatenate([zero, up], 0) + jnp.concatenate([down, zero], 0)
            )
            if j == 0:
                acc = from_left(total)
            elif j == 1:
                acc = acc + total
            else:
                acc = acc + from_right(total)
        pre_ref[f] = acc
        for j, t in enumerate(shifted_transposes(x[f].reshape(PIX, C))):
            xt_ref[j, f] = t


def edge_kernel(core, pre, pair, chip, ws, gp, hid_ref, fac_ref, ht_ref, xe_ref, gt_ref):
    for f in range(2):
        low, high = low_high(core, pair[f, 0], chip[f, 0])
        top = from_left(mm(low, ws[0])) + mm(low, ws[1]) + from_right(mm(low, ws[2]))
        end = from_left(mm(high, ws[6])) + mm(high, ws[7]) + from_right(mm(high, ws[8]))
        value = jnp.concatenate(
            [
                pre[f, 0:COLS] + top,
                pre[f, COLS : 3 * COLS],
                pre[f, 3 * COLS :] + end,
            ],
            0,
        )
        sig = jax.nn.sigmoid(value)
        hidden = (value * sig).astype(BF16)
        hid_ref[f] = hidden.reshape(ROWS, COLS, C)
        fac_ref[f] = sig * (1.0 + value * (1.0 - sig))
        ht_ref[f] = hidden.T
        lows, highs = shifted_transposes(low), shifted_transposes(high)
        for j in range(3):
            xe_ref[j, f, 0] = lows[j]
            xe_ref[j, f, 1] = highs[j]
    gt_ref[0] = mm(ht_ref[0], gp[1])
    gt_ref[1] = mm(ht_ref[0], gp[0]) + mm(ht_ref[1], gp[1])


def grad_kernel(
    core, n, gh, fac, xt, xe, ht, gt, wt, pm,
    gpre_hbm, pair_hbm, keep_ref, send_ref,
    gpre_ref, sems,
):
    def store(tap, value):
        keep_ref[tap] = value[:, : C // 2]
        send_ref[tap] = value[:, C // 2 :].astype(BF16)

    a0, a1 = n[0].reshape(PIX, C), n[1].reshape(PIX, C)
    p0 = mm(a0, pm[...]).astype(BF16)
    p1 = mm(a1, pm[...]).astype(BF16)
    store(9, mm(ht[0], p0) + mm(ht[1], p1))
    store(10, gt[0] + mm(ht[1], p0))
    store(11, gt[1])
    back0 = gh[0] + mm_t(a0, wt[0])
    back1 = gh[1] + mm_t(a0, wt[1]) + mm_t(a1, wt[0])
    grads = []
    for f, back in enumerate((back0, back1)):
        gpre = (back.astype(BF16).astype(F32) * fac[f]).astype(BF16)
        gpre_ref[f] = gpre.reshape(ROWS, COLS, C)
        grads.append(mm(gpre, pm[...]).astype(BF16))
    c = core[0]
    copies = [
        pltpu.make_async_copy(gpre_ref.at[:, pl.ds(3 - 3 * c, 1)], pair_hbm, sems.at[0]),
        pltpu.make_async_copy(gpre_ref, gpre_hbm, sems.at[1]),
    ]
    for copy in copies:
        copy.start()
    for j in range(3):
        for i in range(3):
            total = None
            for f in range(2):
                own = xt[j, f]
                if i == 0:
                    own = jnp.concatenate([xe[j, f, 0], own[:, : 3 * COLS]], 1)
                elif i == 2:
                    own = jnp.concatenate([own[:, COLS:], xe[j, f, 1]], 1)
                part = mm(own, grads[f])
                total = part if total is None else total + part
            store(3 * i + j, total)
    for copy in copies:
        copy.wait()


def pair_kernel(core, keep, got, gpre, out_hbm, chip_ref, out_ref, sems):
    half = C // 4
    rows = gpre.at[:, pl.ds(3 * core[0], 1)]
    copies = [pltpu.make_async_copy(rows, chip_ref, sems.at[6])]
    copies[0].start()
    for p in range(TAPS // 2):
        s0 = keep[2 * p] + got[2 * p].astype(F32)
        s1 = keep[2 * p + 1] + got[2 * p + 1].astype(F32)
        low = jnp.concatenate([s0[:, :half], s1[:, :half]], 1).astype(BF16)
        high = jnp.concatenate([s0[:, half:], s1[:, half:]], 1).astype(BF16)
        for a in range(8):
            out_ref[a, 32 * p : 32 * p + 32] = low[32 * a : 32 * a + 32]
            out_ref[8 + a, 32 * p : 32 * p + 32] = high[32 * a : 32 * a + 32]
        part = pl.ds(32 * p, 32)
        copy = pltpu.make_async_copy(out_ref.at[:, part], out_hbm.at[:, part], sems.at[p])
        copy.start()
        copies.append(copy)
    for copy in copies:
        copy.wait()


def plane_kernel(got, pair, chip, out_ref):
    parts = [got[n].astype(F32) for n in range(16)]
    while len(parts) > 1:
        parts = [parts[n] + parts[n + 1] for n in range(0, len(parts), 2)]
    four, two = parts[0][:128].T, parts[0][128:].T
    wide = jnp.concatenate([four[:64], two[:64], four[64:], two[64:]], 1)
    for z in range(16):
        out_ref[z] = wide[4 * z : 4 * z + 4]


def last_kernel(got, gs_ref, gt_ref):
    total = got[0]
    for n in range(1, 16):
        total = total + got[n]
    for t in range(TAPS):
        at = 32 * (6 * (t % 2) + t // 2)
        if t < 9:
            gs_ref[t] = total[:, at : at + 32]
        else:
            gt_ref[t - 9] = total[:, at : at + 32]


def token_kernel(*refs):
    out_ref = refs[-1]
    out_ref[...] = jnp.zeros(out_ref.shape, F32)


def out_kernel(hid, past, wt, out_ref):
    h0, h1 = hid[0].reshape(PIX, C), hid[1].reshape(PIX, C)
    p0, p1 = past[0].reshape(PIX, C), past[1].reshape(PIX, C)
    first = mm(p0, wt[0]) + mm(p1, wt[1]) + mm(h0, wt[2])
    out_ref[0] = first.astype(BF16).reshape(ROWS, COLS, C)
    second = mm(p1, wt[0]) + mm(h0, wt[1]) + mm(h1, wt[2])
    out_ref[1] = second.astype(BF16).reshape(ROWS, COLS, C)


def back_kernel(core, gpre, pair, chip, ws, token, arrived, out_ref):
    for f in range(2):
        low, high = low_high(core, pair[f, 0], chip[f, 0])
        own = gpre[f].reshape(PIX, C)
        after = jnp.concatenate([own[COLS:], high], 0)
        before = jnp.concatenate([low, own[: 3 * COLS]], 0)
        sums = [
            mm_t(after, ws[j]) + mm_t(own, ws[3 + j]) + mm_t(before, ws[6 + j])
            for j in range(3)
        ]
        total = from_right(sums[0]) + sums[1] + from_left(sums[2])
        out_ref[f] = total.astype(BF16).reshape(ROWS, COLS, C)


SPACE = ("xl", "z", "c")


def steps(count):
    forward = [(i, i + 1) for i in range(count - 1)]
    return forward, [(b, a) for a, b in forward]


def to_pair(rows):
    return lax.ppermute(rows, "c", [(0, 1), (1, 0)])


def to_chip(rows):
    across = [(i, i + 1) for i in range(1, 63, 2)]
    return lax.ppermute(rows, SPACE, across + [(b, a) for a, b in across])


def body(frames_in, w_space, w_time, grad_out):
    forward, backward = steps(8)
    core = lax.axis_index("c").reshape(1)
    order = call(order_kernel, shape((C, C), BF16), HINT, 1 << 17, core)
    rows = shape((2, 1, COLS, C), BF16)
    later = lax.ppermute(grad_out, "tm", backward)
    gh_part, gp, pair, chip = call(
        first_kernel,
        (shape((2, PIX, C), F32), shape((2, PIX, C), BF16), rows, rows),
        4 * TAP_FLOPS,
        4 << 20,
        core, frames_in, grad_out, w_time, order,
    )
    pair, chip = to_pair(pair), to_chip(chip)
    pre_part, xt = call(
        own_kernel,
        (shape((2, PIX, C), F32), shape((3, 2, C, PIX), BF16)),
        9 * TAP_FLOPS,
        4 << 20,
        frames_in, w_space,
    )
    hidden, factor, ht, xe, gt_part = call(
        edge_kernel,
        (
            shape((2, ROWS, COLS, C), BF16),
            shape((2, PIX, C), F32),
            shape((2, C, PIX), BF16),
            shape((3, 2, 2, C, COLS), BF16),
            shape((2, C, C), F32),
        ),
        5 * TAP_FLOPS,
        8 << 20,
        core, pre_part, pair, chip, w_space, gp,
    )
    grad_pre, pair, keep, send = call(
        grad_kernel,
        (
            hbm((2, ROWS, COLS, C), BF16),
            hbm((2, 1, COLS, C), BF16),
            vmem((TAPS, C, C // 2), F32),
            vmem((TAPS, C, C // 2), BF16),
        ),
        15 * TAP_FLOPS,
        10 << 20,
        core, later, gh_part, factor, xt, xe, ht, gt_part, w_time, order,
        hbm_out=(0, 1),
        scratch=[pltpu.VMEM((2, ROWS, COLS, C), BF16), pltpu.SemaphoreType.DMA((2,))],
    )
    got = lax.ppermute(send, "c", [(0, 1), (1, 0)])
    chunks, chip = call(
        pair_kernel,
        (hbm((16, 192, 128), BF16), vmem((2, 1, COLS, C), BF16)),
        1 << 20,
        4 << 20,
        core, keep, got, pltpu.with_memory_space_constraint(grad_pre, pltpu.HBM),
        hbm_in=(3,),
        hbm_out=(0,),
        scratch=[pltpu.VMEM((16, 192, 128), BF16), pltpu.SemaphoreType.DMA((7,))],
    )
    chunks = lax.all_to_all(chunks, ("xl", "tm"), split_axis=0, concat_axis=0, tiled=True)
    pair = to_pair(pair)
    token = call(token_kernel, shape((8, 128), F32), HINT, 1 << 12, pair, chip, hbm_in=(0,))
    chip, token = lax.optimization_barrier((chip, token))
    chip = to_chip(chip)
    arrived = call(token_kernel, shape((8, 128), F32), 0, 1 << 12, chip, pair, hbm_in=(0, 1))
    hidden, arrived = lax.optimization_barrier((hidden, arrived))
    past = lax.ppermute(hidden, "tm", forward)
    chunks, arrived = lax.optimization_barrier((chunks, arrived))
    block_out = call(
        out_kernel,
        shape((2, ROWS, COLS, C), BF16),
        3 * TAP_FLOPS,
        2 << 20,
        hidden, past, w_time,
    )
    grad_in = call(
        back_kernel,
        shape((2, ROWS, COLS, C), BF16),
        9 * TAP_FLOPS,
        4 << 20,
        core, grad_pre, pair, chip, w_space, token, arrived,
    )
    rows = call(plane_kernel, shape((16, 4, 384), F32), 1 << 20, 1 << 20, chunks, pair, chip)
    rows = lax.all_to_all(rows, "z", split_axis=0, concat_axis=0, tiled=True)
    rows, block_out = lax.optimization_barrier((rows, block_out))
    grad_space, grad_time = call(
        last_kernel, (shape((9, 4, 32), F32), shape((3, 4, 32), F32)), 1 << 16, 1 << 18, rows
    )
    return (
        block_out,
        grad_in,
        jnp.transpose(grad_space, (0, 2, 1)),
        jnp.transpose(grad_time, (0, 2, 1)),
    )


def solution(mesh):
    fine = Mesh(mesh.devices.reshape(8, 2, 16, 2), ("tm",) + SPACE)
    in_specs = (P("tm", SPACE, None, None), P(), P(), P("tm", SPACE, None, None))
    out_specs = (
        P("tm", SPACE, None, None),
        P("tm", SPACE, None, None),
        P(None, "tm", SPACE),
        P(None, "tm", SPACE),
    )
    return jax.shard_map(body, mesh=fine, in_specs=in_specs, out_specs=out_specs, check_vma=False)
```
